256 devices in a mesh: span: 64 (over y_lo, x, z), tile: 4 (over y_hi, core).
Axes of the slice: x: 4, y: 4 (y_hi: 2, y_lo: 2; y = y_hi * 2 + y_lo), z: 8, core: 2. Of those that a mesh axis runs over, the one named last changes fastest.
Arguments:
- features: bfloat16 [64, 41, 16, 768], P('span', None, 'tile'), may hold values from -10 to 10
- clip_lengths: int32 [64], replicated, may hold values from 1 to 41, as said below
- slot_table: int32 [64, 41], replicated, may hold values from -1 to 2047, as said below
- gain_one: float32 [384], replicated, may hold values from 0.25 to 1.75
- weight_one: bfloat16 [3, 3, 3, 384, 384], replicated, may hold values from -0.0625 to 0.0625
- gain_two: float32 [384], replicated, may hold values from 0.25 to 1.75
- weight_two: bfloat16 [3, 3, 3, 384, 384], replicated, may hold values from -0.0625 to 0.0625
Outputs:
- decoded: bfloat16 [2048, 16, 768], P('span', 'tile')
The draws below stay inside these ranges and needn't reach their ends.
Inputs may be any that keep to these rules, and one draw needn't show every extreme that they name: `clip_lengths`: the lengths add up to 32 times the number of tenants, and one clip has exactly 41 frames. `slot_table`: entries with f < clip_lengths[t] name every work slot exactly once, so that work slots d * 32 to d * 32 + 32 - 1 (those of index d of span) hold exactly 32 frames; at most 1 frames of one clip fall into the slots of one index of span, and in every draw some clip puts exactly 1 there. Entries with f >= clip_lengths[t] are -1.
All inputs are finite; a program needn't handle non-finite values.
Results may differ from the reference program's by a relative error of at most 0.0038.
Values may be sent and summed in bfloat16 or wider, within the bound.
A program may use at most 128 MiB of HBM per device.

```python
import jax
import jax.numpy as jnp
from jax import lax

C = 384
COLS = 2
MAXF = 41
WSLOT = 32
TENANTS = 64
SLOTS = 2048
ROWS = 16


def plan_tables(key):
    key_spread, key_perm, key_order = jax.random.split(key, 3)
    tenant_count = TENANTS
    deficit = MAXF - WSLOT
    share_each = deficit // (tenant_count - 1)
    extra_count = deficit % (tenant_count - 1)
    position = jnp.arange(tenant_count, dtype=jnp.int32)
    base_length = jnp.where(position < 1 + extra_count, WSLOT - share_each - 1, WSLOT - share_each)
    pair_index = jnp.maximum(position - 1, 0) // 2
    reach_most = min(WSLOT - share_each - 2, MAXF - (WSLOT - share_each))
    amounts = jax.random.randint(key_spread, (tenant_count,), 0, reach_most + 1, dtype=jnp.int32)
    signed = jnp.where((position - 1) % 2 == 0, 1, -1) * amounts[pair_index]
    unpaired = (position == 0) | ((tenant_count - 1) % 2 == 1) & (position == tenant_count - 1)
    lengths_ordered = jnp.where(position == 0, MAXF, base_length + jnp.where(unpaired, 0, signed)).astype(jnp.int32)
    permuted = jax.random.permutation(key_perm, tenant_count)
    lengths = jnp.zeros((tenant_count,), jnp.int32).at[permuted].set(lengths_ordered)
    offsets = jnp.cumsum(lengths) - lengths
    frame_ids = jnp.arange(MAXF, dtype=jnp.int32)
    flat_index = offsets[:, None] + frame_ids[None, :]
    devices = jax.random.permutation(key_order, tenant_count).astype(jnp.int32)
    slot_ids = devices[flat_index % tenant_count] * WSLOT + flat_index // tenant_count
    assigned = jnp.where(frame_ids[None, :] < lengths[:, None], slot_ids, -1)
    return (lengths.astype(jnp.int32), assigned.astype(jnp.int32))


def draw_clip_lengths(key, part):
    shared = plan_tables(key)
    return shared[0]


def draw_slot_table(key, part):
    shared = plan_tables(key)
    return shared[1]


def draw_features(key, part):
    key = jax.random.fold_in(key, 3)
    key_noise, key_chan, key_pixel = jax.random.split(key, 3)
    grid_shape = (TENANTS, MAXF, ROWS, COLS, C)
    channel_scale = jnp.exp(jax.random.uniform(key_chan, (C,), jnp.float32, -1.15, 1.15))
    noise_part = jax.random.normal(key_noise, grid_shape, jnp.float32)
    pixel_scale = jnp.exp(jax.random.uniform(key_pixel, grid_shape[:4] + (1,), jnp.float32, -0.35, 0.35))
    values = noise_part * channel_scale * pixel_scale
    values = jnp.clip(values, -10.0, 10.0)
    return values.reshape(TENANTS, MAXF, ROWS, COLS * C).astype(jnp.bfloat16)


def scatter_about(stream_key, shape, scale, bound, kind=jnp.bfloat16):
    entries = scale * jax.random.normal(stream_key, shape, jnp.float32)
    return jnp.clip(entries, min=-bound, max=bound).astype(kind)


def setup_inputs(seed: int = 0) -> dict:
    key_of = jax.random.split(jax.random.key(seed), 8)
    features = draw_features(jax.random.fold_in(key_of[7], 71), 0)
    clip_lengths = draw_clip_lengths(jax.random.fold_in(key_of[7], 71), 0)
    slot_table = draw_slot_table(jax.random.fold_in(key_of[7], 71), 0)
    gain_one = jnp.clip(1.0 + 0.15 * jax.random.normal(key_of[3], (C,), jnp.float32), 0.25, 1.75)
    weight_one = scatter_about(key_of[4], (3, 3, 3, C, C), (27 * C) ** -0.5, 0.0625)
    gain_two = jnp.clip(1.0 + 0.15 * jax.random.normal(key_of[5], (C,), jnp.float32), 0.25, 1.75)
    weight_two = scatter_about(key_of[6], (3, 3, 3, C, C), (27 * C) ** -0.5, 0.0625)
    return dict(features=features, clip_lengths=clip_lengths, slot_table=slot_table, gain_one=gain_one, weight_one=weight_one, gain_two=gain_two, weight_two=weight_two)


def activate(values, gain_vec):
    channels = gain_vec.shape[0]
    widened = values.astype(jnp.float32)
    shaped = widened.reshape(widened.shape[:-1] + (widened.shape[-1] // channels, channels))
    scaled = shaped * lax.rsqrt(lax.optimization_barrier(jnp.mean(shaped * shaped, axis=-1, keepdims=True)) + 1e-06) * gain_vec
    return jax.nn.silu(scaled).astype(jnp.bfloat16).reshape(values.shape)

def causal_conv(act, weight):
    channels = weight.shape[-1]
    frame_count, row_count, breadth = act.shape
    columns = breadth // channels
    shaped = act.reshape(frame_count, row_count, columns, channels)
    shaped = jnp.pad(shaped, ((0, 0), (1, 1), (1, 1), (0, 0)))
    out_frames = frame_count - 2
    summed = jnp.zeros((out_frames, row_count, columns, channels), jnp.float32)
    for time_tap in range(3):
        for row_tap in range(3):
            for column_tap in range(3):
                window = shaped[time_tap:time_tap + out_frames, row_tap:row_tap + row_count, column_tap:column_tap + columns]
                summed = summed + jnp.einsum('frwc,cd->frwd', window.astype(jnp.float32), weight[time_tap, row_tap, column_tap].astype(jnp.float32))
    return summed.reshape(out_frames, row_count, breadth)

def clip_block(clip_frames, gain_one, weight_one, gain_two, weight_two):
    leading = jnp.zeros((4,) + clip_frames.shape[1:], clip_frames.dtype)
    padded = jnp.concatenate([leading, clip_frames], axis=0)
    act_one = activate(padded, gain_one)
    hidden = causal_conv(act_one, weight_one).astype(jnp.bfloat16)
    act_two = activate(hidden, gain_two)
    branch = causal_conv(act_two, weight_two)
    return (clip_frames.astype(jnp.float32) + branch).astype(jnp.bfloat16)

def reference(features, clip_lengths, slot_table, gain_one, weight_one, gain_two, weight_two):

    def one_clip(clip_frames):
        return clip_block(clip_frames, gain_one, weight_one, gain_two, weight_two)
    results = lax.map(one_clip, features)
    frame_ids = jnp.arange(MAXF, dtype=jnp.int32)
    alive_mask = frame_ids[None, :] < clip_lengths[:, None]
    flat_slots = jnp.where(alive_mask, slot_table, SLOTS).reshape(-1).astype(jnp.int32)
    source = jnp.zeros((SLOTS,), jnp.int32).at[flat_slots].set(jnp.arange(TENANTS * MAXF, dtype=jnp.int32), mode='drop')
    flat_results = results.reshape((TENANTS * MAXF,) + results.shape[2:])
    return flat_results[source]
```

```python
import functools

import jax
import jax.numpy as jnp
from jax import lax
from jax.experimental import pallas as pl
from jax.experimental.pallas import tpu as pltpu
from jax.sharding import PartitionSpec as P

MESH = pl.DeviceIdType.MESH
FRAMES = 41
PAD = 48
ROWS = 4
C = 384
WIDE = 2 * C
WSLOT = 32
SPAN = 64
TILES = 4
TAPS = 9
LANES = 128
GROUPS = WIDE // LANES
F32 = jnp.float32
BF16 = jnp.bfloat16


def activate(values, gain):
    def half(x):
        return jax.nn.silu(x * lax.rsqrt(jnp.mean(x * x, axis=-1, keepdims=True) + 1e-06) * gain)

    return jnp.concatenate([half(values[:, :C]), half(values[:, C:])], axis=1)


def put_shifts(shifted, row, values, own=True):
    frame = lax.broadcasted_iota(jnp.int32, values.shape, 0)
    if own:
        shifted[2, row] = values.astype(BF16)
    shifted[1, row] = jnp.where(frame >= 1, pltpu.roll(values, 1, 0), 0.0).astype(BF16)
    shifted[0, row] = jnp.where(frame >= 2, pltpu.roll(values, 2, 0), 0.0).astype(BF16)


def causal_conv(shifted, weight, total, rows, wait):
    size = rows * PAD
    total[:size] = jnp.zeros((size, WIDE), F32)

    def step(a, carry):
        for b in range(3):
            wait(a * 3 + b)
        lhs = jnp.concatenate([shifted[a, b : b + rows].reshape(size, WIDE) for b in range(3)], axis=1)
        rhs = jnp.concatenate(
            [
                jnp.concatenate([weight[a * 3 + b, C : 3 * C], weight[a * 3 + b, 0 : 2 * C]], axis=1)
                for b in range(3)
            ],
            axis=0,
        )
        total[:size] += jnp.dot(lhs, rhs, preferred_element_type=F32)
        return carry

    lax.fori_loop(0, 3, step, 0)


def kernel(
    feat, slots, gain_one, w_one, gain_two, w_two, out,
    raw, slotv, g1, g2, nat, sh1, sh2, total, v1, v2, send, arrive, pickv, srcv, picks, srcs,
    in_sem, w_sem, smem_sem, halo_send, halo_recv, send_sem, recv_sem,
):
    pos = lax.axis_index("span")
    tile = lax.axis_index("tile")

    inputs = [
        pltpu.make_async_copy(feat, raw, in_sem.at[0]),
        pltpu.make_async_copy(gain_one, g1, in_sem.at[1]),
        pltpu.make_async_copy(slots, slotv, in_sem.at[2]),
        pltpu.make_async_copy(gain_two, g2, in_sem.at[3]),
    ]
    for copy in inputs:
        copy.start()
    for which, (src, dst) in enumerate(((w_one, v1), (w_two, v2))):
        for tap in range(TAPS):
            pltpu.make_async_copy(src.at[tap], dst.at[tap], w_sem.at[which, tap]).start()

    barrier = pltpu.get_barrier_semaphore()

    def greet(k, carry):
        pl.semaphore_signal(
            barrier, inc=1, device_id={"span": lax.rem(pos + k, SPAN), "tile": tile}, device_id_type=MESH
        )
        return carry

    for side in (1, TILES - 1):
        pl.semaphore_signal(
            barrier, inc=1, device_id={"span": pos, "tile": lax.rem(tile + side, TILES)}, device_id_type=MESH
        )
    lax.fori_loop(1, SPAN, greet, 0)

    inputs[0].wait()
    inputs[1].wait()
    for f in range(FRAMES):
        values = raw[f].astype(F32)
        for g in range(GROUPS):
            nat[g, ROWS * f : ROWS * (f + 1), :] = values[:, g * LANES : (g + 1) * LANES]
    nat[:, ROWS * FRAMES :, :] = jnp.zeros((GROUPS, ROWS * (PAD - FRAMES), LANES), F32)
    for r in range(ROWS):
        values = jnp.concatenate([nat[g, pl.ds(r, PAD, stride=ROWS), :] for g in range(GROUPS)], axis=1)
        put_shifts(sh1, 2 + r, activate(values, g1[...].reshape(1, C)))

    pl.semaphore_wait(barrier, SPAN + 1)

    down = pltpu.make_async_remote_copy(
        src_ref=sh1.at[2, pl.ds(4, 2)], dst_ref=sh1.at[2, pl.ds(0, 2)],
        send_sem=halo_send.at[0], recv_sem=halo_recv.at[0],
        device_id={"span": pos, "tile": lax.rem(tile + 1, TILES)}, device_id_type=MESH,
    )
    up = pltpu.make_async_remote_copy(
        src_ref=sh1.at[2, pl.ds(2, 2)], dst_ref=sh1.at[2, pl.ds(6, 2)],
        send_sem=halo_send.at[1], recv_sem=halo_recv.at[1],
        device_id={"span": pos, "tile": lax.rem(tile + TILES - 1, TILES)}, device_id_type=MESH,
    )

    @pl.when(tile < TILES - 1)
    def _():
        down.start()

    @pl.when(tile > 0)
    def _():
        up.start()

    inputs[2].wait()
    inputs[3].wait()
    table = slotv[...]
    lane = lax.broadcasted_iota(jnp.int32, (FRAMES, SPAN), 1)
    column = jnp.sum(jnp.where(lane == pos, table, 0), axis=1, keepdims=True)
    target = jnp.where(column >= 0, column // WSLOT, -1)
    wide_lane = lax.broadcasted_iota(jnp.int32, (FRAMES, 128), 1)
    frame = lax.broadcasted_iota(jnp.int32, (FRAMES, 128), 0)
    pick = jnp.max(jnp.where(target == wide_lane, frame, 0), axis=0, keepdims=True)
    pickv[...] = jnp.broadcast_to(pick, (8, 128))
    wanted = pos * WSLOT + lax.broadcasted_iota(jnp.int32, (WSLOT, SPAN), 0)
    clip = lax.broadcasted_iota(jnp.int32, (WSLOT, SPAN), 1)
    found = jnp.zeros((WSLOT, SPAN), jnp.int32)
    for f in range(FRAMES):
        found = jnp.where(table[f : f + 1, :] == wanted, clip, found)
    srcv[...] = jnp.broadcast_to(jnp.max(found, axis=1, keepdims=True), (WSLOT, 128))
    to_smem = [
        pltpu.make_async_copy(pickv, picks, smem_sem.at[0]),
        pltpu.make_async_copy(srcv, srcs, smem_sem.at[1]),
    ]
    for copy in to_smem:
        copy.start()

    @pl.when(tile > 0)
    def _():
        down.wait_recv()

    @pl.when(tile == 0)
    def _():
        sh1[2, 0:2] = jnp.zeros((2, PAD, WIDE), BF16)

    @pl.when(tile < TILES - 1)
    def _():
        up.wait_recv()

    @pl.when(tile == TILES - 1)
    def _():
        sh1[2, 6:8] = jnp.zeros((2, PAD, WIDE), BF16)

    for row in (0, 1, 6, 7):
        put_shifts(sh1, row, sh1[2, row].astype(F32), own=False)

    def wait_for(which, src, dst):
        def wait(tap):
            pltpu.make_async_copy(src.at[tap], dst.at[tap], w_sem.at[which, tap]).wait()

        return wait

    causal_conv(sh1, v1, total, 6, wait_for(0, w_one, v1))
    for q in range(6):
        values = activate(total[q * PAD : (q + 1) * PAD, :].astype(BF16).astype(F32), g2[...].reshape(1, C))
        if q == 0:
            values = jnp.where(tile == 0, 0.0, values)
        if q == 5:
            values = jnp.where(tile == TILES - 1, 0.0, values)
        put_shifts(sh2, q, values)
    causal_conv(sh2, v2, total, ROWS, wait_for(1, w_two, v2))
    for r in range(ROWS):
        for g in range(GROUPS):
            nat[g, pl.ds(r, PAD, stride=ROWS), :] += total[
                r * PAD : (r + 1) * PAD, g * LANES : (g + 1) * LANES
            ]
    for f in range(FRAMES):
        frame_rows = [nat[g, ROWS * f : ROWS * (f + 1), :] for g in range(GROUPS)]
        raw[f] = jnp.concatenate(frame_rows, axis=1).astype(BF16)

    for copy in to_smem:
        copy.wait()

    def parcel(dest):
        return raw[picks[0, dest]]

    arrive[pos] = parcel(pos)

    def post(k, carry):
        dest = lax.rem(pos + k, SPAN)
        send[dest] = parcel(dest)
        pltpu.make_async_remote_copy(
            src_ref=send.at[dest], dst_ref=arrive.at[pos], send_sem=send_sem, recv_sem=recv_sem,
            device_id={"span": dest, "tile": tile}, device_id_type=MESH,
        ).start()
        return carry

    lax.fori_loop(1, SPAN, post, 0)

    @pl.when(tile < TILES - 1)
    def _():
        down.wait_send()

    @pl.when(tile > 0)
    def _():
        up.wait_send()

    every = pl.ds(0, SPAN - 1)
    pltpu.make_async_copy(send.at[every], send.at[every], send_sem).wait()
    pltpu.make_async_copy(arrive.at[every], arrive.at[every], recv_sem).wait()

    def place(j, carry):
        out[j] = arrive[srcs[j, 0]]
        return carry

    lax.fori_loop(0, WSLOT, place, 0)


def local(features, clip_lengths, slot_table, gain_one, weight_one, gain_two, weight_two):
    del clip_lengths
    hbm = pl.BlockSpec(memory_space=pl.ANY)
    return pl.pallas_call(
        kernel,
        out_shape=jax.ShapeDtypeStruct((WSLOT, ROWS, WIDE), BF16),
        in_specs=[hbm] * 6,
        out_specs=pl.BlockSpec(memory_space=pltpu.VMEM),
        scratch_shapes=[
            pltpu.VMEM((FRAMES, ROWS, WIDE), BF16),
            pltpu.VMEM((FRAMES, SPAN), jnp.int32),
            pltpu.VMEM((C,), F32),
            pltpu.VMEM((C,), F32),
            pltpu.VMEM((GROUPS, ROWS * PAD, LANES), F32),
            pltpu.VMEM((3, 8, PAD, WIDE), BF16),
            pltpu.VMEM((3, 6, PAD, WIDE), BF16),
            pltpu.VMEM((6 * PAD, WIDE), F32),
            pltpu.VMEM((TAPS, 3 * C, C), BF16),
            pltpu.VMEM((TAPS, 3 * C, C), BF16),
            pltpu.VMEM((SPAN, ROWS, WIDE), BF16),
            pltpu.VMEM((SPAN, ROWS, WIDE), BF16),
            pltpu.VMEM((8, 128), jnp.int32),
            pltpu.VMEM((WSLOT, 128), jnp.int32),
            pltpu.SMEM((8, 128), jnp.int32),
            pltpu.SMEM((WSLOT, 128), jnp.int32),
            pltpu.SemaphoreType.DMA((4,)),
            pltpu.SemaphoreType.DMA((2, TAPS)),
            pltpu.SemaphoreType.DMA((2,)),
            pltpu.SemaphoreType.DMA((2,)),
            pltpu.SemaphoreType.DMA((2,)),
            pltpu.SemaphoreType.DMA,
            pltpu.SemaphoreType.DMA,
        ],
        compiler_params=pltpu.CompilerParams(
            collective_id=0, has_side_effects=True, vmem_limit_bytes=60 * 1024 * 1024
        ),
    )(
        features.reshape(FRAMES, ROWS, WIDE),
        slot_table.T,
        gain_one,
        weight_one.reshape(TAPS, 3 * C, C),
        gain_two,
        weight_two.reshape(TAPS, 3 * C, C),
    )


def solution(mesh):
    return jax.shard_map(
        local,
        mesh=mesh,
        in_specs=(P("span", None, "tile", None), P(), P(), P(), P(), P(), P()),
        out_specs=P("span", "tile", None),
        check_vma=False,
    )
```

```python
import functools

import jax
import jax.numpy as jnp
from jax import lax
from jax.experimental import pallas as pl
from jax.experimental.pallas import tpu as pltpu
from jax.sharding import PartitionSpec as P

MESH = pl.DeviceIdType.MESH
FRAMES = 41
PAD = 48
ROWS = 4
C = 384
WIDE = 2 * C
WSLOT = 32
SPAN = 64
TILES = 4
TAPS = 9
LANES = 128
GROUPS = WIDE // LANES
F32 = jnp.float32
BF16 = jnp.bfloat16


def activate(values, gain):
    def half(x):
        return jax.nn.silu(x * lax.rsqrt(jnp.mean(x * x, axis=-1, keepdims=True) + 1e-06) * gain)

    return jnp.concatenate([half(values[:, :C]), half(values[:, C:])], axis=1)


def put_shifts(shifted, row, values):
    frame = lax.broadcasted_iota(jnp.int32, values.shape, 0)
    shifted[2, row] = values.astype(BF16)
    shifted[1, row] = jnp.where(frame >= 1, pltpu.roll(values, 1, 0), 0.0).astype(BF16)
    shifted[0, row] = jnp.where(frame >= 2, pltpu.roll(values, 2, 0), 0.0).astype(BF16)


def causal_conv(shifted, first, rows, weight, total):
    size = rows * PAD
    lhs = jnp.concatenate(
        [shifted[a, first + b : first + b + rows].reshape(size, WIDE) for a in range(3) for b in range(3)], axis=1
    )
    for block in range(3):
        rhs = []
        for tap in range(TAPS):
            if block == 0:
                rhs.append(weight[tap, C:, 0:256])
            elif block == 1:
                rhs.append(jnp.concatenate([weight[tap, C:, 256:], weight[tap, : 2 * C, :128]], axis=1))
            else:
                rhs.append(weight[tap, : 2 * C, 128:])
        total[:size, block * 256 : (block + 1) * 256] = jnp.dot(
            lhs, jnp.concatenate(rhs, axis=0), preferred_element_type=F32
        )


def kernel(
    feat, slots, gain_one, w_one, gain_two, w_two, out,
    raw, slotv, g1, g2, nat, mix, sh1, sh2, near, far, total, v1, v2, block, send, arrive, pickv, srcv, picks, srcs,
    in_sem, w_sem, smem_sem, halo_send, halo_recv, send_sem, recv_sem,
):
    pos = lax.axis_index("span")
    tile = lax.axis_index("tile")
    flip = tile // 2
    edge = jnp.where((tile == 0) | (tile == TILES - 1), 1, 0)
    partner = tile + 1 - 2 * lax.rem(tile, 2)
    opposite = TILES - 1 - tile

    def physical(row):
        return row + flip * (ROWS - 1 - 2 * row)

    inputs = [
        pltpu.make_async_copy(feat, raw, in_sem.at[0]),
        pltpu.make_async_copy(gain_one, g1, in_sem.at[1]),
        pltpu.make_async_copy(slots, slotv, in_sem.at[2]),
        pltpu.make_async_copy(gain_two, g2, in_sem.at[3]),
    ]
    for copy in inputs:
        copy.start()
    weights = []
    for which, (src, dst) in enumerate(((w_one, v1), (w_two, v2))):
        for a in range(3):
            for b in range(3):
                tap = a * 3 + b + flip * (2 - 2 * b)
                weights.append(pltpu.make_async_copy(src.at[tap], dst.at[a * 3 + b], w_sem.at[which, a * 3 + b]))
    for copy in weights:
        copy.start()

    barrier = pltpu.get_barrier_semaphore()

    def greet(k, carry):
        pl.semaphore_signal(
            barrier, inc=1, device_id={"span": lax.rem(pos + k, SPAN), "tile": tile}, device_id_type=MESH
        )
        return carry

    for other in (partner, opposite):
        pl.semaphore_signal(barrier, inc=1, device_id={"span": pos, "tile": other}, device_id_type=MESH)
    lax.fori_loop(1, SPAN, greet, 0)

    inputs[0].wait()
    inputs[1].wait()
    for f in range(FRAMES):
        values = raw[f].astype(F32)
        for g in range(GROUPS):
            nat[g, ROWS * f : ROWS * (f + 1), :] = values[:, g * LANES : (g + 1) * LANES]
    nat[:, ROWS * FRAMES :, :] = jnp.zeros((GROUPS, ROWS * (PAD - FRAMES), LANES), F32)

    def own_row(step):
        row = lax.rem(step + 2 * edge, ROWS)
        at = pl.ds(physical(row), PAD, stride=ROWS)
        values = jnp.concatenate([nat[g, at, :] for g in range(GROUPS)], axis=1)
        put_shifts(sh1, 2 + row, activate(values, g1[...].reshape(1, C)))

    own_row(0)
    own_row(1)
    pl.semaphore_wait(barrier, SPAN + 1)
    to_near = pltpu.make_async_remote_copy(
        src_ref=sh1.at[2, pl.ds(2 + 2 * edge, 2)], dst_ref=near, send_sem=halo_send.at[0], recv_sem=halo_recv.at[0],
        device_id={"span": pos, "tile": partner}, device_id_type=MESH,
    )
    to_near.start()
    own_row(2)
    own_row(3)
    to_far = pltpu.make_async_remote_copy(
        src_ref=sh1.at[2, pl.ds(4, 2)], dst_ref=far, send_sem=halo_send.at[1], recv_sem=halo_recv.at[1],
        device_id={"span": pos, "tile": opposite}, device_id_type=MESH,
    )

    @pl.when(edge == 0)
    def _():
        to_far.start()

    inputs[2].wait()
    inputs[3].wait()
    table = slotv[...]
    lane = lax.broadcasted_iota(jnp.int32, (FRAMES, SPAN), 1)
    column = jnp.sum(jnp.where(lane == pos, table, 0), axis=1, keepdims=True)
    target = jnp.where(column >= 0, column // WSLOT, -1)
    wide_lane = lax.broadcasted_iota(jnp.int32, (FRAMES, 128), 1)
    frame = lax.broadcasted_iota(jnp.int32, (FRAMES, 128), 0)
    pick = jnp.max(jnp.where(target == wide_lane, frame, 0), axis=0, keepdims=True)
    pickv[...] = jnp.broadcast_to(pick, (8, 128))
    wanted = pos * WSLOT + lax.broadcasted_iota(jnp.int32, (WSLOT, SPAN), 0)
    clip = lax.broadcasted_iota(jnp.int32, (WSLOT, SPAN), 1)
    found = jnp.zeros((WSLOT, SPAN), jnp.int32)
    for f in range(FRAMES):
        found = jnp.where(table[f : f + 1, :] == wanted, clip, found)
    srcv[...] = jnp.broadcast_to(jnp.max(found, axis=1, keepdims=True), (WSLOT, 128))
    to_smem = [
        pltpu.make_async_copy(pickv, picks, smem_sem.at[0]),
        pltpu.make_async_copy(srcv, srcs, smem_sem.at[1]),
    ]
    for copy in to_smem:
        copy.start()

    @pl.when(edge == 1)
    def _():
        sh1[:, 0:2] = jnp.zeros((3, 2, PAD, WIDE), BF16)

    @pl.when(edge == 0)
    def _():
        to_near.wait_recv()
        for row in range(2):
            put_shifts(sh1, row, near[row].astype(F32))

    def hidden_rows(first, rows):
        for i in range(rows):
            values = activate(total[i * PAD : (i + 1) * PAD, :].astype(BF16).astype(F32), g2[...].reshape(1, C))
            if first + i == 0:
                values = jnp.where(edge == 1, 0.0, values)
            put_shifts(sh2, first + i, values)

    def emit(half):
        part = half + flip * (1 - 2 * half)
        for i in range(2):
            row = physical(2 * half + i)
            for g in range(GROUPS):
                mix[g, pl.ds(lax.rem(row, 2), PAD, stride=2), :] = (
                    nat[g, pl.ds(row, PAD, stride=ROWS), :]
                    + total[i * PAD : (i + 1) * PAD, g * LANES : (g + 1) * LANES]
                )
        for f in range(FRAMES):
            block[f] = jnp.concatenate([mix[g, 2 * f : 2 * f + 2, :] for g in range(GROUPS)], axis=1).astype(BF16)
        arrive[part, pos] = block[picks[0, pos]]

        def post(k, carry):
            dest = lax.rem(pos + k, SPAN)
            send[part, dest] = block[picks[0, dest]]
            pltpu.make_async_remote_copy(
                src_ref=send.at[part, dest], dst_ref=arrive.at[part, pos],
                send_sem=send_sem.at[half], recv_sem=recv_sem.at[half],
                device_id={"span": dest, "tile": tile}, device_id_type=MESH,
            ).start()
            return carry

        lax.fori_loop(1, SPAN, post, 0)

    for copy in weights[:TAPS]:
        copy.wait()
    causal_conv(sh1, 0, 4, v1, total)
    hidden_rows(0, 4)
    for copy in weights[TAPS:]:
        copy.wait()
    causal_conv(sh2, 0, 2, v2, total)
    for copy in to_smem:
        copy.wait()
    emit(0)

    @pl.when(edge == 1)
    def _():
        to_near.wait_recv()
        for row in range(2):
            put_shifts(sh1, 6 + row, near[row].astype(F32))

    @pl.when(edge == 0)
    def _():
        to_far.wait_recv()
        for row in range(2):
            put_shifts(sh1, 7 - row, far[row].astype(F32))

    causal_conv(sh1, 4, 2, v1, total)
    hidden_rows(4, 2)
    causal_conv(sh2, 2, 2, v2, total)
    emit(1)

    to_near.wait_send()

    @pl.when(edge == 0)
    def _():
        to_far.wait_send()

    every = pl.ds(0, SPAN - 1)
    for half in range(2):
        pltpu.make_async_copy(send.at[half, every], send.at[half, every], send_sem.at[half]).wait()
        pltpu.make_async_copy(arrive.at[half, every], arrive.at[half, every], recv_sem.at[half]).wait()

    def place(j, carry):
        clip = srcs[j, 0]
        out[j] = jnp.concatenate([arrive[0, clip], arrive[1, clip]], axis=0)
        return carry

    lax.fori_loop(0, WSLOT, place, 0)


def local(features, clip_lengths, slot_table, gain_one, weight_one, gain_two, weight_two):
    del clip_lengths
    hbm = pl.BlockSpec(memory_space=pl.ANY)
    return pl.pallas_call(
        kernel,
        out_shape=jax.ShapeDtypeStruct((WSLOT, ROWS, WIDE), BF16),
        in_specs=[hbm] * 6,
        out_specs=pl.BlockSpec(memory_space=pltpu.VMEM),
        scratch_shapes=[
            pltpu.VMEM((FRAMES, ROWS, WIDE), BF16),
            pltpu.VMEM((FRAMES, SPAN), jnp.int32),
            pltpu.VMEM((C,), F32),
            pltpu.VMEM((C,), F32),
            pltpu.VMEM((GROUPS, ROWS * PAD, LANES), F32),
            pltpu.VMEM((GROUPS, 2 * PAD, LANES), F32),
            pltpu.VMEM((3, 8, PAD, WIDE), BF16),
            pltpu.VMEM((3, 6, PAD, WIDE), BF16),
            pltpu.VMEM((2, PAD, WIDE), BF16),
            pltpu.VMEM((2, PAD, WIDE), BF16),
            pltpu.VMEM((4 * PAD, WIDE), F32),
            pltpu.VMEM((TAPS, 3 * C, C), BF16),
            pltpu.VMEM((TAPS, 3 * C, C), BF16),
            pltpu.VMEM((FRAMES, 2, WIDE), BF16),
            pltpu.VMEM((2, SPAN, 2, WIDE), BF16),
            pltpu.VMEM((2, SPAN, 2, WIDE), BF16),
            pltpu.VMEM((8, 128), jnp.int32),
            pltpu.VMEM((WSLOT, 128), jnp.int32),
            pltpu.SMEM((8, 128), jnp.int32),
            pltpu.SMEM((WSLOT, 128), jnp.int32),
            pltpu.SemaphoreType.DMA((4,)),
            pltpu.SemaphoreType.DMA((2, TAPS)),
            pltpu.SemaphoreType.DMA((2,)),
            pltpu.SemaphoreType.DMA((2,)),
            pltpu.SemaphoreType.DMA((2,)),
            pltpu.SemaphoreType.DMA((2,)),
            pltpu.SemaphoreType.DMA((2,)),
        ],
        compiler_params=pltpu.CompilerParams(
            collective_id=0, has_side_effects=True, vmem_limit_bytes=60 * 1024 * 1024
        ),
    )(
        features.reshape(FRAMES, ROWS, WIDE),
        slot_table.T,
        gain_one,
        weight_one.reshape(TAPS, 3 * C, C),
        gain_two,
        weight_two.reshape(TAPS, 3 * C, C),
    )


def solution(mesh):
    return jax.shard_map(
        local,
        mesh=mesh,
        in_specs=(P("span", None, "tile", None), P(), P(), P(), P(), P(), P()),
        out_specs=P("span", "tile", None),
        check_vma=False,
    )
```

```python
import functools

import jax
import jax.numpy as jnp
from jax import lax
from jax.experimental import pallas as pl
from jax.experimental.pallas import tpu as pltpu
from jax.sharding import PartitionSpec as P

MESH = pl.DeviceIdType.MESH
FRAMES = 41
PAD = 48
ROWS = 4
C = 384
WIDE = 2 * C
WSLOT = 32
SPAN = 64
TILES = 4
TAPS = 9
ACROSS = 4
DEPTH = 8
ORDER = [
    (dy, dx, dz)
    for dy, dx in ((1, 2), (0, 2), (1, 1), (1, 3), (0, 1), (0, 3), (1, 0), (0, 0))
    for dz in (4, 3, 5, 2, 6, 1, 7, 0)
][: SPAN - 1]
EACH = 8
LANES = 128
GROUPS = WIDE // LANES
F32 = jnp.float32
BF16 = jnp.bfloat16


def activate(values, gain):
    def half(x):
        return jax.nn.silu(x * lax.rsqrt(jnp.mean(x * x, axis=-1, keepdims=True) + 1e-06) * gain)

    return jnp.concatenate([half(values[:, :C]), half(values[:, C:])], axis=1)


def put_shifts(shifted, row, values):
    frame = lax.broadcasted_iota(jnp.int32, values.shape, 0)
    shifted[2, row] = values.astype(BF16)
    shifted[1, row] = jnp.where(frame >= 1, pltpu.roll(values, 1, 0), 0.0).astype(BF16)
    shifted[0, row] = jnp.where(frame >= 2, pltpu.roll(values, 2, 0), 0.0).astype(BF16)


def product(shifted, pieces, rows, weight, total, start, add=False, between=None):
    size = rows * PAD
    lhs = jnp.concatenate(
        [shifted[a, first : first + rows].reshape(size, WIDE) for a, b, first in pieces], axis=1
    )
    for block in range(3):
        rhs = []
        for a, b, _ in pieces:
            tap = a * 3 + b
            if block == 0:
                rhs.append(weight[tap, C:, 0:256])
            elif block == 1:
                rhs.append(jnp.concatenate([weight[tap, C:, 256:], weight[tap, : 2 * C, :128]], axis=1))
            else:
                rhs.append(weight[tap, : 2 * C, 128:])
        result = jnp.dot(lhs, jnp.concatenate(rhs, axis=0), preferred_element_type=F32)
        at = (slice(start * PAD, start * PAD + size), slice(block * 256, (block + 1) * 256))
        total[at] = total[at] + result if add else result
        if between is not None:
            between()


def taps(row_taps, first):
    return [(a, b, first + b) for a in range(3) for b in row_taps]


def kernel(
    feat, slots, gain_one, w_one, gain_two, w_two, out,
    raw, slotv, g1, g2, nat, mix, sh1, sh2, near, far, total, v1, v2, block, send, arrive, pickv, srcv, picks, srcs,
    in_sem, w_sem, smem_sem, halo_send, halo_recv, send_sem, recv_sem,
):
    pos = lax.axis_index("span")
    tile = lax.axis_index("tile")
    flip = tile // 2
    edge = jnp.where((tile == 0) | (tile == TILES - 1), 1, 0)
    partner = tile + 1 - 2 * lax.rem(tile, 2)
    opposite = TILES - 1 - tile

    def physical(row):
        return row + flip * (ROWS - 1 - 2 * row)

    inputs = [
        pltpu.make_async_copy(feat, raw, in_sem.at[0]),
        pltpu.make_async_copy(gain_one, g1, in_sem.at[1]),
        pltpu.make_async_copy(slots, slotv, in_sem.at[2]),
        pltpu.make_async_copy(gain_two, g2, in_sem.at[3]),
    ]
    for copy in inputs:
        copy.start()
    weights = []
    for which, (src, dst) in enumerate(((w_one, v1), (w_two, v2))):
        for a in range(3):
            for b in range(3):
                tap = a * 3 + b + flip * (2 - 2 * b)
                weights.append(pltpu.make_async_copy(src.at[tap], dst.at[a * 3 + b], w_sem.at[which, a * 3 + b]))
    for copy in weights:
        copy.start()

    barrier = pltpu.get_barrier_semaphore()

    def greet(k, carry):
        pl.semaphore_signal(
            barrier, inc=1, device_id={"span": lax.rem(pos + k, SPAN), "tile": tile}, device_id_type=MESH
        )
        return carry

    for other in (partner, opposite):
        pl.semaphore_signal(barrier, inc=1, device_id={"span": pos, "tile": other}, device_id_type=MESH)
    lax.fori_loop(1, SPAN, greet, 0)

    inputs[0].wait()
    inputs[1].wait()
    for f in range(FRAMES):
        values = raw[f].astype(F32)
        for g in range(GROUPS):
            nat[g, ROWS * f : ROWS * (f + 1), :] = values[:, g * LANES : (g + 1) * LANES]
    nat[:, ROWS * FRAMES :, :] = jnp.zeros((GROUPS, ROWS * (PAD - FRAMES), LANES), F32)

    def own_row(step):
        row = lax.rem(step + 2 * edge, ROWS)
        at = pl.ds(physical(row), PAD, stride=ROWS)
        values = jnp.concatenate([nat[g, at, :] for g in range(GROUPS)], axis=1)
        put_shifts(sh1, 2 + row, activate(values, g1[...].reshape(1, C)))

    own_row(0)
    own_row(1)
    pl.semaphore_wait(barrier, SPAN + 1)
    to_near = pltpu.make_async_remote_copy(
        src_ref=sh1.at[2, pl.ds(2 + 2 * edge, 2)], dst_ref=near, send_sem=halo_send.at[0], recv_sem=halo_recv.at[0],
        device_id={"span": pos, "tile": partner}, device_id_type=MESH,
    )
    to_near.start()
    own_row(2)
    own_row(3)
    to_far = pltpu.make_async_remote_copy(
        src_ref=sh1.at[2, pl.ds(4, 2)], dst_ref=far, send_sem=halo_send.at[1], recv_sem=halo_recv.at[1],
        device_id={"span": pos, "tile": opposite}, device_id_type=MESH,
    )

    @pl.when(edge == 0)
    def _():
        to_far.start()

    inputs[2].wait()
    inputs[3].wait()
    table = slotv[...]
    lane = lax.broadcasted_iota(jnp.int32, (FRAMES, SPAN), 1)
    column = jnp.sum(jnp.where(lane == pos, table, 0), axis=1, keepdims=True)
    target = jnp.where(column >= 0, column // WSLOT, -1)
    wide_lane = lax.broadcasted_iota(jnp.int32, (FRAMES, 128), 1)
    frame = lax.broadcasted_iota(jnp.int32, (FRAMES, 128), 0)
    pick = jnp.max(jnp.where(target == wide_lane, frame, 0), axis=0, keepdims=True)
    pickv[...] = jnp.broadcast_to(pick, (8, 128))
    wanted = pos * WSLOT + lax.broadcasted_iota(jnp.int32, (WSLOT, SPAN), 0)
    clip = lax.broadcasted_iota(jnp.int32, (WSLOT, SPAN), 1)
    found = jnp.zeros((WSLOT, SPAN), jnp.int32)
    for f in range(FRAMES):
        found = jnp.where(table[f : f + 1, :] == wanted, clip, found)
    srcv[...] = jnp.broadcast_to(jnp.max(found, axis=1, keepdims=True), (WSLOT, 128))
    to_smem = [
        pltpu.make_async_copy(pickv, picks, smem_sem.at[0]),
        pltpu.make_async_copy(srcv, srcs, smem_sem.at[1]),
    ]
    for copy in to_smem:
        copy.start()

    def hidden_row(row, start):
        values = activate(total[start * PAD : (start + 1) * PAD, :].astype(BF16).astype(F32), g2[...].reshape(1, C))
        if row == 0:
            values = jnp.where(edge == 1, 0.0, values)
        put_shifts(sh2, row, values)

    def prepare(half):
        for i in range(2):
            row = physical(2 * half + i)
            for g in range(GROUPS):
                mix[g, pl.ds(lax.rem(row, 2), PAD, stride=2), :] = (
                    nat[g, pl.ds(row, PAD, stride=ROWS), :]
                    + total[i * PAD : (i + 1) * PAD, g * LANES : (g + 1) * LANES]
                )
        for f in range(FRAMES):
            block[half, f] = jnp.concatenate([mix[g, 2 * f : 2 * f + 2, :] for g in range(GROUPS)], axis=1).astype(BF16)
        arrive[half + flip * (1 - 2 * half), pos] = block[half, picks[0, pos]]

    z, x, y = lax.rem(pos, DEPTH), lax.rem(pos // DEPTH, ACROSS), pos // (DEPTH * ACROSS)

    def posts(half, count):
        part = half + flip * (1 - 2 * half)
        done = 0
        for dy, dx, dz in ORDER:
            dest = (lax.rem(y + dy, 2) * ACROSS + lax.rem(x + dx, ACROSS)) * DEPTH + lax.rem(z + dz, DEPTH)
            send[part, dest] = block[half, picks[0, dest]]
            pltpu.make_async_remote_copy(
                src_ref=send.at[part, dest], dst_ref=arrive.at[part, pos],
                send_sem=send_sem.at[half], recv_sem=recv_sem.at[half],
                device_id={"span": dest, "tile": tile}, device_id_type=MESH,
            ).start()
            done += 1
            if done % count == 0:
                yield
        while True:
            yield

    for copy in weights[:TAPS]:
        copy.wait()
    product(sh1, taps((2,), 0), 4, v1, total, 0)
    product(sh1, taps((0, 1), 2), 2, v1, total, 2, add=True)
    hidden_row(2, 2)
    hidden_row(3, 3)

    @pl.when(edge == 1)
    def _():
        sh1[:, 0:2] = jnp.zeros((3, 2, PAD, WIDE), BF16)

    @pl.when(edge == 0)
    def _():
        to_near.wait_recv()
        for row in range(2):
            put_shifts(sh1, row, near[row].astype(F32))

    product(sh1, taps((0, 1), 0), 2, v1, total, 0, add=True)
    hidden_row(0, 0)
    hidden_row(1, 1)
    for copy in weights[TAPS:]:
        copy.wait()
    product(sh2, taps((0, 1, 2), 0), 2, v2, total, 0)
    for copy in to_smem:
        copy.wait()
    prepare(0)

    @pl.when(edge == 1)
    def _():
        to_near.wait_recv()
        for row in range(2):
            put_shifts(sh1, 6 + row, near[row].astype(F32))

    @pl.when(edge == 0)
    def _():
        to_far.wait_recv()
        for row in range(2):
            put_shifts(sh1, 7 - row, far[row].astype(F32))

    first_half = posts(0, EACH)

    def some():
        next(first_half)

    some()
    product(sh1, taps((0, 1, 2), 4), 2, v1, total, 0, between=some)
    hidden_row(4, 0)
    some()
    hidden_row(5, 1)
    product(sh2, taps((0, 1, 2), 2), 2, v2, total, 0, between=some)
    prepare(1)
    next(posts(1, SPAN))

    to_near.wait_send()

    @pl.when(edge == 0)
    def _():
        to_far.wait_send()

    every = pl.ds(0, SPAN - 1)
    for half in range(2):
        pltpu.make_async_copy(send.at[half, every], send.at[half, every], send_sem.at[half]).wait()
        pltpu.make_async_copy(arrive.at[half, every], arrive.at[half, every], recv_sem.at[half]).wait()

    def place(j, carry):
        clip = srcs[j, 0]
        out[j] = jnp.concatenate([arrive[0, clip], arrive[1, clip]], axis=0)
        return carry

    lax.fori_loop(0, WSLOT, place, 0)


def local(features, clip_lengths, slot_table, gain_one, weight_one, gain_two, weight_two):
    del clip_lengths
    hbm = pl.BlockSpec(memory_space=pltpu.HBM)
    operands = [
        features.reshape(FRAMES, ROWS, WIDE),
        slot_table.T,
        gain_one,
        weight_one.reshape(TAPS, 3 * C, C),
        gain_two,
        weight_two.reshape(TAPS, 3 * C, C),
    ]
    operands = [pltpu.with_memory_space_constraint(x, pltpu.HBM) for x in operands]
    return pl.pallas_call(
        kernel,
        out_shape=pltpu.VMEM((WSLOT, ROWS, WIDE), BF16),
        in_specs=[hbm] * 6,
        out_specs=pl.BlockSpec(memory_space=pltpu.VMEM),
        scratch_shapes=[
            pltpu.VMEM((FRAMES, ROWS, WIDE), BF16),
            pltpu.VMEM((FRAMES, SPAN), jnp.int32),
            pltpu.VMEM((C,), F32),
            pltpu.VMEM((C,), F32),
            pltpu.VMEM((GROUPS, ROWS * PAD, LANES), F32),
            pltpu.VMEM((GROUPS, 2 * PAD, LANES), F32),
            pltpu.VMEM((3, 8, PAD, WIDE), BF16),
            pltpu.VMEM((3, 6, PAD, WIDE), BF16),
            pltpu.VMEM((2, PAD, WIDE), BF16),
            pltpu.VMEM((2, PAD, WIDE), BF16),
            pltpu.VMEM((4 * PAD, WIDE), F32),
            pltpu.VMEM((TAPS, 3 * C, C), BF16),
            pltpu.VMEM((TAPS, 3 * C, C), BF16),
            pltpu.VMEM((2, FRAMES, 2, WIDE), BF16),
            pltpu.VMEM((2, SPAN, 2, WIDE), BF16),
            pltpu.VMEM((2, SPAN, 2, WIDE), BF16),
            pltpu.VMEM((8, 128), jnp.int32),
            pltpu.VMEM((WSLOT, 128), jnp.int32),
            pltpu.SMEM((8, 128), jnp.int32),
            pltpu.SMEM((WSLOT, 128), jnp.int32),
            pltpu.SemaphoreType.DMA((4,)),
            pltpu.SemaphoreType.DMA((2, TAPS)),
            pltpu.SemaphoreType.DMA((2,)),
            pltpu.SemaphoreType.DMA((2,)),
            pltpu.SemaphoreType.DMA((2,)),
            pltpu.SemaphoreType.DMA((2,)),
            pltpu.SemaphoreType.DMA((2,)),
        ],
        compiler_params=pltpu.CompilerParams(
            collective_id=0, has_side_effects=True, vmem_limit_bytes=48 * 1024 * 1024
        ),
    )(*operands)


def solution(mesh):
    return jax.shard_map(
        local,
        mesh=mesh,
        in_specs=(P("span", None, "tile", None), P(), P(), P(), P(), P(), P()),
        out_specs=P("span", "tile", None),
        check_vma=False,
    )
```

```python
import functools

import jax
import jax.numpy as jnp
from jax import lax
from jax.experimental import pallas as pl
from jax.experimental.pallas import tpu as pltpu
from jax.sharding import PartitionSpec as P

MESH = pl.DeviceIdType.MESH
FRAMES = 41
PAD = 48
ROWS = 4
C = 384
WIDE = 2 * C
WSLOT = 32
SPAN = 64
TILES = 4
TAPS = 9
ACROSS = 4
DEPTH = 8
ORDER = [
    (dy, dx, dz)
    for dy, dx in ((1, 2), (0, 2), (1, 1), (1, 3), (0, 1), (0, 3), (1, 0), (0, 0))
    for dz in (4, 3, 5, 2, 6, 1, 7, 0)
][: SPAN - 1]
LANES = 128
GROUPS = WIDE // LANES
F32 = jnp.float32
BF16 = jnp.bfloat16


def activate(values, gain):
    def half(x):
        return jax.nn.silu(x * lax.rsqrt(jnp.mean(x * x, axis=-1, keepdims=True) + 1e-06) * gain)

    return jnp.concatenate([half(values[:, :C]), half(values[:, C:])], axis=1)


def put_shifts(shifted, row, values):
    frame = lax.broadcasted_iota(jnp.int32, values.shape, 0)
    shifted[2, row] = values.astype(BF16)
    shifted[1, row] = jnp.where(frame >= 1, pltpu.roll(values, 1, 0), 0.0).astype(BF16)
    shifted[0, row] = jnp.where(frame >= 2, pltpu.roll(values, 2, 0), 0.0).astype(BF16)


def product(shifted, pieces, rows, weight, total, start, add=False):
    size = rows * PAD
    lhs = jnp.concatenate(
        [shifted[a, first : first + rows].reshape(size, WIDE) for a, b, first in pieces], axis=1
    )
    for block in range(3):
        rhs = []
        for a, b, _ in pieces:
            tap = a * 3 + b
            if block == 0:
                rhs.append(weight[tap, C:, 0:256])
            elif block == 1:
                rhs.append(jnp.concatenate([weight[tap, C:, 256:], weight[tap, : 2 * C, :128]], axis=1))
            else:
                rhs.append(weight[tap, : 2 * C, 128:])
        result = jnp.dot(lhs, jnp.concatenate(rhs, axis=0), preferred_element_type=F32)
        at = (slice(start * PAD, start * PAD + size), slice(block * 256, (block + 1) * 256))
        total[at] = total[at] + result if add else result


def taps(row_taps, first):
    return [(a, b, first + b) for a in range(3) for b in row_taps]


def kernel(
    feat, slots, gain_one, w_one, gain_two, w_two, out,
    raw, slotv, g1, g2, nat, mix, sh1, sh2, near, far, total, v1, v2, block, send, arrive, pickv, srcv, picks, srcs,
    in_sem, w_sem, smem_sem, halo_send, halo_recv, send_sem, recv_sem,
):
    pos = lax.axis_index("span")
    tile = lax.axis_index("tile")
    flip = tile // 2
    edge = jnp.where((tile == 0) | (tile == TILES - 1), 1, 0)
    partner = tile + 1 - 2 * lax.rem(tile, 2)
    opposite = TILES - 1 - tile

    def physical(row):
        return row + flip * (ROWS - 1 - 2 * row)

    inputs = [
        pltpu.make_async_copy(feat, raw, in_sem.at[0]),
        pltpu.make_async_copy(gain_one, g1, in_sem.at[1]),
        pltpu.make_async_copy(slots, slotv, in_sem.at[2]),
        pltpu.make_async_copy(gain_two, g2, in_sem.at[3]),
    ]
    for copy in inputs:
        copy.start()
    weights = []
    for which, (src, dst) in enumerate(((w_one, v1), (w_two, v2))):
        for a in range(3):
            for b in range(3):
                tap = a * 3 + b + flip * (2 - 2 * b)
                weights.append(pltpu.make_async_copy(src.at[tap], dst.at[a * 3 + b], w_sem.at[which, a * 3 + b]))
    for copy in weights:
        copy.start()

    barrier = pltpu.get_barrier_semaphore()

    def greet(k, carry):
        pl.semaphore_signal(
            barrier, inc=1, device_id={"span": lax.rem(pos + k, SPAN), "tile": tile}, device_id_type=MESH
        )
        return carry

    for other in (partner, opposite):
        pl.semaphore_signal(barrier, inc=1, device_id={"span": pos, "tile": other}, device_id_type=MESH)
    lax.fori_loop(1, SPAN, greet, 0)

    inputs[0].wait()
    inputs[1].wait()
    for f in range(FRAMES):
        values = raw[f].astype(F32)
        for g in range(GROUPS):
            nat[g, ROWS * f : ROWS * (f + 1), :] = values[:, g * LANES : (g + 1) * LANES]
    nat[:, ROWS * FRAMES :, :] = jnp.zeros((GROUPS, ROWS * (PAD - FRAMES), LANES), F32)

    def own_row(step):
        row = lax.rem(step + 2 * edge, ROWS)
        at = pl.ds(physical(row), PAD, stride=ROWS)
        values = jnp.concatenate([nat[g, at, :] for g in range(GROUPS)], axis=1)
        put_shifts(sh1, 2 + row, activate(values, g1[...].reshape(1, C)))

    own_row(0)
    own_row(1)
    pl.semaphore_wait(barrier, SPAN + 1)
    to_near = pltpu.make_async_remote_copy(
        src_ref=sh1.at[2, pl.ds(2 + 2 * edge, 2)], dst_ref=near, send_sem=halo_send.at[0], recv_sem=halo_recv.at[0],
        device_id={"span": pos, "tile": partner}, device_id_type=MESH,
    )
    to_near.start()
    own_row(2)
    own_row(3)
    to_far = pltpu.make_async_remote_copy(
        src_ref=sh1.at[2, pl.ds(4, 2)], dst_ref=far, send_sem=halo_send.at[1], recv_sem=halo_recv.at[1],
        device_id={"span": pos, "tile": opposite}, device_id_type=MESH,
    )

    @pl.when(edge == 0)
    def _():
        to_far.start()

    inputs[2].wait()
    inputs[3].wait()
    table = slotv[...]
    lane = lax.broadcasted_iota(jnp.int32, (FRAMES, SPAN), 1)
    column = jnp.sum(jnp.where(lane == pos, table, 0), axis=1, keepdims=True)
    target = jnp.where(column >= 0, column // WSLOT, -1)
    wide_lane = lax.broadcasted_iota(jnp.int32, (FRAMES, 128), 1)
    frame = lax.broadcasted_iota(jnp.int32, (FRAMES, 128), 0)
    pick = jnp.max(jnp.where(target == wide_lane, frame, 0), axis=0, keepdims=True)
    pickv[...] = jnp.broadcast_to(pick, (8, 128))
    wanted = pos * WSLOT + lax.broadcasted_iota(jnp.int32, (WSLOT, SPAN), 0)
    clip = lax.broadcasted_iota(jnp.int32, (WSLOT, SPAN), 1)
    found = jnp.zeros((WSLOT, SPAN), jnp.int32)
    for f in range(FRAMES):
        found = jnp.where(table[f : f + 1, :] == wanted, clip, found)
    srcv[...] = jnp.broadcast_to(jnp.max(found, axis=1, keepdims=True), (WSLOT, 128))
    to_smem = [
        pltpu.make_async_copy(pickv, picks, smem_sem.at[0]),
        pltpu.make_async_copy(srcv, srcs, smem_sem.at[1]),
    ]
    for copy in to_smem:
        copy.start()

    def hidden_row(row, start):
        values = activate(total[start * PAD : (start + 1) * PAD, :].astype(BF16).astype(F32), g2[...].reshape(1, C))
        if row == 0:
            values = jnp.where(edge == 1, 0.0, values)
        put_shifts(sh2, row, values)

    def prepare(half):
        for i in range(2):
            row = physical(2 * half + i)
            for g in range(GROUPS):
                mix[g, pl.ds(lax.rem(row, 2), PAD, stride=2), :] = (
                    nat[g, pl.ds(row, PAD, stride=ROWS), :]
                    + total[i * PAD : (i + 1) * PAD, g * LANES : (g + 1) * LANES]
                )
        for f in range(FRAMES):
            block[half, f] = jnp.concatenate([mix[g, 2 * f : 2 * f + 2, :] for g in range(GROUPS)], axis=1).astype(BF16)
        arrive[half + flip * (1 - 2 * half), pos] = block[half, picks[0, pos]]

    z, x, y = lax.rem(pos, DEPTH), lax.rem(pos // DEPTH, ACROSS), pos // (DEPTH * ACROSS)

    def post(half):
        part = half + flip * (1 - 2 * half)
        for dy, dx, dz in ORDER:
            dest = (lax.rem(y + dy, 2) * ACROSS + lax.rem(x + dx, ACROSS)) * DEPTH + lax.rem(z + dz, DEPTH)
            send[part, dest] = block[half, picks[0, dest]]
            pltpu.make_async_remote_copy(
                src_ref=send.at[part, dest], dst_ref=arrive.at[part, pos],
                send_sem=send_sem.at[half], recv_sem=recv_sem.at[half],
                device_id={"span": dest, "tile": tile}, device_id_type=MESH,
            ).start()

    for copy in weights[:TAPS]:
        copy.wait()
    product(sh1, taps((2,), 0), 4, v1, total, 0)
    product(sh1, taps((0, 1), 2), 2, v1, total, 2, add=True)
    hidden_row(2, 2)
    hidden_row(3, 3)

    @pl.when(edge == 1)
    def _():
        sh1[:, 0:2] = jnp.zeros((3, 2, PAD, WIDE), BF16)

    @pl.when(edge == 0)
    def _():
        to_near.wait_recv()
        for row in range(2):
            put_shifts(sh1, row, near[row].astype(F32))

    product(sh1, taps((0, 1), 0), 2, v1, total, 0, add=True)
    hidden_row(0, 0)
    hidden_row(1, 1)
    for copy in weights[TAPS:]:
        copy.wait()
    product(sh2, taps((0, 1, 2), 0), 2, v2, total, 0)
    for copy in to_smem:
        copy.wait()
    prepare(0)
    post(0)

    @pl.when(edge == 1)
    def _():
        to_near.wait_recv()
        for row in range(2):
            put_shifts(sh1, 6 + row, near[row].astype(F32))

    @pl.when(edge == 0)
    def _():
        to_far.wait_recv()
        for row in range(2):
            put_shifts(sh1, 7 - row, far[row].astype(F32))

    product(sh1, taps((0, 1, 2), 4), 2, v1, total, 0)
    hidden_row(4, 0)
    hidden_row(5, 1)
    product(sh2, taps((0, 1, 2), 2), 2, v2, total, 0)
    prepare(1)
    post(1)

    to_near.wait_send()

    @pl.when(edge == 0)
    def _():
        to_far.wait_send()

    every = pl.ds(0, SPAN - 1)
    for half in range(2):
        pltpu.make_async_copy(send.at[half, every], send.at[half, every], send_sem.at[half]).wait()
        pltpu.make_async_copy(arrive.at[half, every], arrive.at[half, every], recv_sem.at[half]).wait()

    def place(j, carry):
        clip = srcs[j, 0]
        out[j] = jnp.concatenate([arrive[0, clip], arrive[1, clip]], axis=0)
        return carry

    lax.fori_loop(0, WSLOT, place, 0)


def local(features, clip_lengths, slot_table, gain_one, weight_one, gain_two, weight_two):
    del clip_lengths
    hbm = pl.BlockSpec(memory_space=pltpu.HBM)
    operands = [
        features.reshape(FRAMES, ROWS, WIDE),
        slot_table.T,
        gain_one,
        weight_one.reshape(TAPS, 3 * C, C),
        gain_two,
        weight_two.reshape(TAPS, 3 * C, C),
    ]
    operands = [pltpu.with_memory_space_constraint(x, pltpu.HBM) for x in operands]
    return pl.pallas_call(
        kernel,
        out_shape=pltpu.VMEM((WSLOT, ROWS, WIDE), BF16),
        in_specs=[hbm] * 6,
        out_specs=pl.BlockSpec(memory_space=pltpu.VMEM),
        scratch_shapes=[
            pltpu.VMEM((FRAMES, ROWS, WIDE), BF16),
            pltpu.VMEM((FRAMES, SPAN), jnp.int32),
            pltpu.VMEM((C,), F32),
            pltpu.VMEM((C,), F32),
            pltpu.VMEM((GROUPS, ROWS * PAD, LANES), F32),
            pltpu.VMEM((GROUPS, 2 * PAD, LANES), F32),
            pltpu.VMEM((3, 8, PAD, WIDE), BF16),
            pltpu.VMEM((3, 6, PAD, WIDE), BF16),
            pltpu.VMEM((2, PAD, WIDE), BF16),
            pltpu.VMEM((2, PAD, WIDE), BF16),
            pltpu.VMEM((4 * PAD, WIDE), F32),
            pltpu.VMEM((TAPS, 3 * C, C), BF16),
            pltpu.VMEM((TAPS, 3 * C, C), BF16),
            pltpu.VMEM((2, FRAMES, 2, WIDE), BF16),
            pltpu.VMEM((2, SPAN, 2, WIDE), BF16),
            pltpu.VMEM((2, SPAN, 2, WIDE), BF16),
            pltpu.VMEM((8, 128), jnp.int32),
            pltpu.VMEM((WSLOT, 128), jnp.int32),
            pltpu.SMEM((8, 128), jnp.int32),
            pltpu.SMEM((WSLOT, 128), jnp.int32),
            pltpu.SemaphoreType.DMA((4,)),
            pltpu.SemaphoreType.DMA((2, TAPS)),
            pltpu.SemaphoreType.DMA((2,)),
            pltpu.SemaphoreType.DMA((2,)),
            pltpu.SemaphoreType.DMA((2,)),
            pltpu.SemaphoreType.DMA((2,)),
            pltpu.SemaphoreType.DMA((2,)),
        ],
        compiler_params=pltpu.CompilerParams(
            collective_id=0, has_side_effects=True, vmem_limit_bytes=48 * 1024 * 1024
        ),
    )(*operands)


def solution(mesh):
    return jax.shard_map(
        local,
        mesh=mesh,
        in_specs=(P("span", None, "tile", None), P(), P(), P(), P(), P(), P()),
        out_specs=P("span", "tile", None),
        check_vma=False,
    )
```

```python
import functools

import jax
import jax.numpy as jnp
from jax import lax
from jax.experimental import pallas as pl
from jax.experimental.pallas import tpu as pltpu
from jax.sharding import PartitionSpec as P

MESH = pl.DeviceIdType.MESH
FRAMES = 41
PAD = 48
ROWS = 4
C = 384
WIDE = 2 * C
WSLOT = 32
SPAN = 64
TILES = 4
TAPS = 9
ACROSS = 4
DEPTH = 8
ORDER = [
    (dy, dx, dz)
    for dy, dx in ((1, 2), (0, 2), (1, 1), (1, 3), (0, 1), (0, 3), (1, 0), (0, 0))
    for dz in (4, 3, 5, 2, 6, 1, 7, 0)
][: SPAN - 1]
LANES = 128
GROUPS = WIDE // LANES
F32 = jnp.float32
BF16 = jnp.bfloat16


def activate(values, gain):
    def half(x):
        u = x * lax.rsqrt(jnp.mean(x * x, axis=-1, keepdims=True) + 1e-06) * gain
        half_u = 0.5 * u
        return half_u + half_u * jnp.tanh(half_u)

    return jnp.concatenate([half(values[:, :C]), half(values[:, C:])], axis=1)


def put_shifts(shifted, row, values):
    frame = lax.broadcasted_iota(jnp.int32, values.shape, 0)
    shifted[2, row] = values.astype(BF16)
    shifted[1, row] = jnp.where(frame >= 1, pltpu.roll(values, 1, 0), 0.0).astype(BF16)
    shifted[0, row] = jnp.where(frame >= 2, pltpu.roll(values, 2, 0), 0.0).astype(BF16)


def product(shifted, pieces, rows, weight, total, start, add=False):
    size = rows * PAD
    lhs = jnp.concatenate(
        [shifted[a, first : first + rows].reshape(size, WIDE) for a, b, first in pieces], axis=1
    )
    for block in range(3):
        rhs = []
        for a, b, _ in pieces:
            tap = a * 3 + b
            if block == 0:
                rhs.append(weight[tap, C:, 0:256])
            elif block == 1:
                rhs.append(jnp.concatenate([weight[tap, C:, 256:], weight[tap, : 2 * C, :128]], axis=1))
            else:
                rhs.append(weight[tap, : 2 * C, 128:])
        result = jnp.dot(lhs, jnp.concatenate(rhs, axis=0), preferred_element_type=F32)
        at = (slice(start * PAD, start * PAD + size), slice(block * 256, (block + 1) * 256))
        total[at] = total[at] + result if add else result


def taps(row_taps, first):
    return [(a, b, first + b) for a in range(3) for b in row_taps]


def kernel(
    feat, slots, gain_one, w_one, gain_two, w_two, out,
    raw, slotv, g1, g2, nat, mix, sh1, sh2, near, far, total, v1, v2, block, send, arrive_one, arrive_two, pickv, srcv, picks, srcs,
    in_sem, w_sem, smem_sem, halo_send, halo_recv, send_sem, recv_sem, lines_sem, planes_sem,
):
    pos = lax.axis_index("span")
    tile = lax.axis_index("tile")
    flip = tile // 2
    arrive = (arrive_one, arrive_two)
    edge = jnp.where((tile == 0) | (tile == TILES - 1), 1, 0)
    partner = tile + 1 - 2 * lax.rem(tile, 2)
    opposite = TILES - 1 - tile

    def physical(row):
        return row + flip * (ROWS - 1 - 2 * row)

    inputs = [
        pltpu.make_async_copy(feat, raw, in_sem.at[0]),
        pltpu.make_async_copy(gain_one, g1, in_sem.at[1]),
        pltpu.make_async_copy(slots, slotv, in_sem.at[2]),
        pltpu.make_async_copy(gain_two, g2, in_sem.at[3]),
    ]
    weights = []
    for which, (src, dst) in enumerate(((w_one, v1), (w_two, v2))):
        for a in range(3):
            for b in range(3):
                tap = a * 3 + b + flip * (2 - 2 * b)
                weights.append(pltpu.make_async_copy(src.at[tap], dst.at[a * 3 + b], w_sem.at[which, a * 3 + b]))
    for copy in inputs[:2]:
        copy.start()

    z, x, y = lax.rem(pos, DEPTH), lax.rem(pos // DEPTH, ACROSS), pos // (DEPTH * ACROSS)

    def shifted_by(dy, dx, dz):
        return (lax.rem(y + dy, 2) * ACROSS + lax.rem(x + dx, ACROSS)) * DEPTH + lax.rem(z + dz, DEPTH)

    barrier = pltpu.get_barrier_semaphore()
    along_z = [shifted_by(0, 0, k) for k in range(1, DEPTH)]
    along_x = [shifted_by(0, k, 0) for k in range(1, ACROSS)]
    along_y = [shifted_by(1, 0, 0)]
    for other in (partner, opposite):
        pl.semaphore_signal(barrier, inc=1, device_id={"span": pos, "tile": other}, device_id_type=MESH)
    for other in along_z + along_x + along_y:
        pl.semaphore_signal(barrier, inc=1, device_id={"span": other, "tile": tile}, device_id_type=MESH)
    for copy in weights[:TAPS] + inputs[2:] + weights[TAPS:]:
        copy.start()

    inputs[0].wait()
    inputs[1].wait()
    for f in range(FRAMES):
        values = raw[f].astype(F32)
        for g in range(GROUPS):
            nat[g, ROWS * f : ROWS * (f + 1), :] = values[:, g * LANES : (g + 1) * LANES]
    nat[:, ROWS * FRAMES :, :] = jnp.zeros((GROUPS, ROWS * (PAD - FRAMES), LANES), F32)

    def own_row(step):
        row = lax.rem(step + 2 * edge, ROWS)
        at = pl.ds(physical(row), PAD, stride=ROWS)
        values = jnp.concatenate([nat[g, at, :] for g in range(GROUPS)], axis=1)
        put_shifts(sh1, 2 + row, activate(values, g1[...].reshape(1, C)))

    own_row(0)
    own_row(1)
    pl.semaphore_wait(barrier, 2 + len(along_z) + len(along_x) + len(along_y))
    to_near = pltpu.make_async_remote_copy(
        src_ref=sh1.at[2, pl.ds(2 + 2 * edge, 2)], dst_ref=near, send_sem=halo_send.at[0], recv_sem=halo_recv.at[0],
        device_id={"span": pos, "tile": partner}, device_id_type=MESH,
    )
    to_near.start()
    for other in along_x:
        pl.semaphore_signal(lines_sem, inc=1, device_id={"span": other, "tile": tile}, device_id_type=MESH)
    own_row(2)
    own_row(3)
    to_far = pltpu.make_async_remote_copy(
        src_ref=sh1.at[2, pl.ds(4, 2)], dst_ref=far, send_sem=halo_send.at[1], recv_sem=halo_recv.at[1],
        device_id={"span": pos, "tile": opposite}, device_id_type=MESH,
    )

    @pl.when(edge == 0)
    def _():
        to_far.start()

    inputs[2].wait()
    inputs[3].wait()
    table = slotv[...]
    lane = lax.broadcasted_iota(jnp.int32, (FRAMES, SPAN), 1)
    column = jnp.sum(jnp.where(lane == pos, table, 0), axis=1, keepdims=True)
    target = jnp.where(column >= 0, column // WSLOT, -1)
    wide_lane = lax.broadcasted_iota(jnp.int32, (FRAMES, 128), 1)
    frame = lax.broadcasted_iota(jnp.int32, (FRAMES, 128), 0)
    pick = jnp.max(jnp.where(target == wide_lane, frame, 0), axis=0, keepdims=True)
    pickv[...] = jnp.broadcast_to(pick, (8, 128))
    wanted = pos * WSLOT + lax.broadcasted_iota(jnp.int32, (WSLOT, SPAN), 0)
    clip = lax.broadcasted_iota(jnp.int32, (WSLOT, SPAN), 1)
    found = jnp.zeros((WSLOT, SPAN), jnp.int32)
    for f in range(FRAMES):
        found = jnp.where(table[f : f + 1, :] == wanted, clip, found)
    srcv[...] = jnp.broadcast_to(jnp.max(found, axis=1, keepdims=True), (WSLOT, 128))
    to_smem = [
        pltpu.make_async_copy(pickv, picks, smem_sem.at[0]),
        pltpu.make_async_copy(srcv, srcs, smem_sem.at[1]),
    ]
    for copy in to_smem:
        copy.start()

    def hidden_row(row, start):
        values = activate(total[start * PAD : (start + 1) * PAD, :].astype(BF16).astype(F32), g2[...].reshape(1, C))
        if row == 0:
            values = jnp.where(edge == 1, 0.0, values)
        put_shifts(sh2, row, values)

    def prepare(half):
        for i in range(2):
            row = physical(2 * half + i)
            for g in range(GROUPS):
                mix[g, pl.ds(lax.rem(row, 2), PAD, stride=2), :] = (
                    nat[g, pl.ds(row, PAD, stride=ROWS), :]
                    + total[i * PAD : (i + 1) * PAD, g * LANES : (g + 1) * LANES]
                )
        for f in range(FRAMES):
            block[half, f] = jnp.concatenate([mix[g, 2 * f : 2 * f + 2, :] for g in range(GROUPS)], axis=1).astype(BF16)
        arrive[half][pos] = block[half, picks[0, pos]]

    def post(half):
        for dy, dx, dz in ORDER:
            dest = shifted_by(dy, dx, dz)
            send[half, dest] = block[half, picks[0, dest]]
            pltpu.make_async_remote_copy(
                src_ref=send.at[half, dest], dst_ref=arrive[half].at[pos],
                send_sem=send_sem.at[half], recv_sem=recv_sem.at[half],
                device_id={"span": dest, "tile": tile}, device_id_type=MESH,
            ).start()

    for copy in weights[:TAPS]:
        copy.wait()
    product(sh1, taps((2,), 0), 4, v1, total, 0)
    pl.semaphore_wait(lines_sem, len(along_x))
    for other in along_y:
        pl.semaphore_signal(planes_sem, inc=1, device_id={"span": other, "tile": tile}, device_id_type=MESH)

    @pl.when(edge == 1)
    def _():
        sh1[:, 0:2] = jnp.zeros((3, 2, PAD, WIDE), BF16)

    @pl.when(edge == 0)
    def _():
        to_near.wait_recv()
        for row in range(2):
            put_shifts(sh1, row, near[row].astype(F32))

    product(sh1, taps((0, 1), 0), 4, v1, total, 0, add=True)
    for row in range(4):
        hidden_row(row, row)
    for copy in weights[TAPS:]:
        copy.wait()
    product(sh2, taps((0, 1, 2), 0), 2, v2, total, 0)
    for copy in to_smem:
        copy.wait()
    prepare(0)
    pl.semaphore_wait(planes_sem, len(along_y))
    post(0)

    @pl.when(edge == 1)
    def _():
        to_near.wait_recv()
        for row in range(2):
            put_shifts(sh1, 6 + row, near[row].astype(F32))

    @pl.when(edge == 0)
    def _():
        to_far.wait_recv()
        for row in range(2):
            put_shifts(sh1, 7 - row, far[row].astype(F32))

    product(sh1, taps((0, 1, 2), 4), 2, v1, total, 0)
    hidden_row(4, 0)
    hidden_row(5, 1)
    product(sh2, taps((0, 1, 2), 2), 2, v2, total, 0)
    prepare(1)
    post(1)

    to_near.wait_send()

    @pl.when(edge == 0)
    def _():
        to_far.wait_send()

    every = pl.ds(0, SPAN - 1)
    for half in range(2):
        pltpu.make_async_copy(send.at[half, every], send.at[half, every], send_sem.at[half]).wait()
        pltpu.make_async_copy(arrive[half].at[every], arrive[half].at[every], recv_sem.at[half]).wait()
        for part in range(2):

            @pl.when(flip == (half + part) % 2)
            def _(half=half, part=part):
                for j in range(WSLOT):
                    out[j, 2 * part : 2 * part + 2] = arrive[half][srcs[j, 0]]


def local(features, clip_lengths, slot_table, gain_one, weight_one, gain_two, weight_two):
    del clip_lengths
    hbm = pl.BlockSpec(memory_space=pltpu.HBM)
    operands = [
        features.reshape(FRAMES, ROWS, WIDE),
        slot_table.T,
        gain_one,
        weight_one.reshape(TAPS, 3 * C, C),
        gain_two,
        weight_two.reshape(TAPS, 3 * C, C),
    ]
    operands = [pltpu.with_memory_space_constraint(x, pltpu.HBM) for x in operands]
    return pl.pallas_call(
        kernel,
        out_shape=pltpu.VMEM((WSLOT, ROWS, WIDE), BF16),
        in_specs=[hbm] * 6,
        out_specs=pl.BlockSpec(memory_space=pltpu.VMEM),
        scratch_shapes=[
            pltpu.VMEM((FRAMES, ROWS, WIDE), BF16),
            pltpu.VMEM((FRAMES, SPAN), jnp.int32),
            pltpu.VMEM((C,), F32),
            pltpu.VMEM((C,), F32),
            pltpu.VMEM((GROUPS, ROWS * PAD, LANES), F32),
            pltpu.VMEM((GROUPS, 2 * PAD, LANES), F32),
            pltpu.VMEM((3, 8, PAD, WIDE), BF16),
            pltpu.VMEM((3, 6, PAD, WIDE), BF16),
            pltpu.VMEM((2, PAD, WIDE), BF16),
            pltpu.VMEM((2, PAD, WIDE), BF16),
            pltpu.VMEM((4 * PAD, WIDE), F32),
            pltpu.VMEM((TAPS, 3 * C, C), BF16),
            pltpu.VMEM((TAPS, 3 * C, C), BF16),
            pltpu.VMEM((2, FRAMES, 2, WIDE), BF16),
            pltpu.VMEM((2, SPAN, 2, WIDE), BF16),
            pltpu.VMEM((SPAN, 2, WIDE), BF16),
            pltpu.VMEM((SPAN, 2, WIDE), BF16),
            pltpu.VMEM((8, 128), jnp.int32),
            pltpu.VMEM((WSLOT, 128), jnp.int32),
            pltpu.SMEM((8, 128), jnp.int32),
            pltpu.SMEM((WSLOT, 128), jnp.int32),
            pltpu.SemaphoreType.DMA((4,)),
            pltpu.SemaphoreType.DMA((2, TAPS)),
            pltpu.SemaphoreType.DMA((2,)),
            pltpu.SemaphoreType.DMA((2,)),
            pltpu.SemaphoreType.DMA((2,)),
            pltpu.SemaphoreType.DMA((2,)),
            pltpu.SemaphoreType.DMA((2,)),
            pltpu.SemaphoreType.REGULAR,
            pltpu.SemaphoreType.REGULAR,
        ],
        compiler_params=pltpu.CompilerParams(
            collective_id=0, has_side_effects=True, vmem_limit_bytes=48 * 1024 * 1024
        ),
    )(*operands)


def solution(mesh):
    return jax.shard_map(
        local,
        mesh=mesh,
        in_specs=(P("span", None, "tile", None), P(), P(), P(), P(), P(), P()),
        out_specs=P("span", "tile", None),
        check_vma=False,
    )
```

```python
import functools

import jax
import jax.numpy as jnp
from jax import lax
from jax.experimental import pallas as pl
from jax.experimental.pallas import tpu as pltpu
from jax.sharding import PartitionSpec as P

MESH = pl.DeviceIdType.MESH
FRAMES = 41
PAD = 48
ROWS = 4
C = 384
WIDE = 2 * C
WSLOT = 32
SPAN = 64
TILES = 4
TAPS = 9
ACROSS = 4
DEPTH = 8
XY = ((1, 2), (0, 2), (1, 1), (1, 3), (0, 1), (0, 3), (1, 0), (0, 0))
ORDER = [(dy, dx, dz) for dy, dx in XY for dz in (4, 3, 5, 2, 6, 1, 7)] + [(dy, dx, 0) for dy, dx in XY[:-1]]
LANES = 128
GROUPS = WIDE // LANES
F32 = jnp.float32
BF16 = jnp.bfloat16


def activate(values, gain):
    def half(x):
        u = x * lax.rsqrt(jnp.mean(x * x, axis=-1, keepdims=True) + 1e-06) * gain
        half_u = 0.5 * u
        return half_u + half_u * jnp.tanh(half_u)

    return jnp.concatenate([half(values[:, :C]), half(values[:, C:])], axis=1)


def put_shifts(shifted, row, values):
    frame = lax.broadcasted_iota(jnp.int32, values.shape, 0)
    shifted[2, row] = values.astype(BF16)
    shifted[1, row] = jnp.where(frame >= 1, pltpu.roll(values, 1, 0), 0.0).astype(BF16)
    shifted[0, row] = jnp.where(frame >= 2, pltpu.roll(values, 2, 0), 0.0).astype(BF16)


def product(shifted, pieces, rows, weight, total, start, add=False):
    size = rows * PAD
    lhs = jnp.concatenate(
        [shifted[a, first : first + rows].reshape(size, WIDE) for a, b, first in pieces], axis=1
    )
    for block in range(3):
        rhs = []
        for a, b, _ in pieces:
            tap = a * 3 + b
            if block == 0:
                rhs.append(weight[tap, C:, 0:256])
            elif block == 1:
                rhs.append(jnp.concatenate([weight[tap, C:, 256:], weight[tap, : 2 * C, :128]], axis=1))
            else:
                rhs.append(weight[tap, : 2 * C, 128:])
        result = jnp.dot(lhs, jnp.concatenate(rhs, axis=0), preferred_element_type=F32)
        at = (slice(start * PAD, start * PAD + size), slice(block * 256, (block + 1) * 256))
        total[at] = total[at] + result if add else result


def taps(row_taps, first):
    return [(a, b, first + b) for a in range(3) for b in row_taps]


def kernel(
    feat, slots, gain_one, w_one, gain_two, w_two, out,
    raw, slotv, g1, g2, nat, mix, sh1, sh2, near, far, total, v1, v2, block, send, arrive_one, arrive_two, pickv, srcv, picks, srcs,
    in_sem, w_sem, smem_sem, halo_send, halo_recv, send_sem, recv_sem, lines_sem, planes_sem,
):
    pos = lax.axis_index("span")
    tile = lax.axis_index("tile")
    flip = tile // 2
    arrive = (arrive_one, arrive_two)
    edge = jnp.where((tile == 0) | (tile == TILES - 1), 1, 0)
    partner = tile + 1 - 2 * lax.rem(tile, 2)
    opposite = TILES - 1 - tile

    def physical(row):
        return row + flip * (ROWS - 1 - 2 * row)

    inputs = [
        pltpu.make_async_copy(feat, raw, in_sem.at[0]),
        pltpu.make_async_copy(gain_one, g1, in_sem.at[1]),
        pltpu.make_async_copy(slots, slotv, in_sem.at[2]),
        pltpu.make_async_copy(gain_two, g2, in_sem.at[3]),
    ]
    weights = []
    for which, (src, dst) in enumerate(((w_one, v1), (w_two, v2))):
        for a in range(3):
            for b in range(3):
                tap = a * 3 + b + flip * (2 - 2 * b)
                weights.append(pltpu.make_async_copy(src.at[tap], dst.at[a * 3 + b], w_sem.at[which, a * 3 + b]))
    for copy in inputs[:2]:
        copy.start()

    z, x, y = lax.rem(pos, DEPTH), lax.rem(pos // DEPTH, ACROSS), pos // (DEPTH * ACROSS)

    def shifted_by(dy, dx, dz):
        return (lax.rem(y + dy, 2) * ACROSS + lax.rem(x + dx, ACROSS)) * DEPTH + lax.rem(z + dz, DEPTH)

    barrier = pltpu.get_barrier_semaphore()
    along_z = [shifted_by(0, 0, k) for k in range(1, DEPTH)]
    along_x = [shifted_by(0, k, 0) for k in range(1, ACROSS)]
    along_y = [shifted_by(1, 0, 0)]
    for other in (partner, opposite):
        pl.semaphore_signal(barrier, inc=1, device_id={"span": pos, "tile": other}, device_id_type=MESH)
    for other in along_z + along_x + along_y:
        pl.semaphore_signal(barrier, inc=1, device_id={"span": other, "tile": tile}, device_id_type=MESH)
    ahead, after = weights[2:TAPS:3] + weights[0:TAPS:3], weights[1:TAPS:3]
    for copy in ahead + after + inputs[2:]:
        copy.start()

    inputs[0].wait()
    inputs[1].wait()
    for f in range(FRAMES):
        values = raw[f].astype(F32)
        for g in range(GROUPS):
            nat[g, ROWS * f : ROWS * (f + 1), :] = values[:, g * LANES : (g + 1) * LANES]
    nat[:, ROWS * FRAMES :, :] = jnp.zeros((GROUPS, ROWS * (PAD - FRAMES), LANES), F32)

    def own_row(step):
        row = lax.rem(step + 2 * edge, ROWS)
        at = pl.ds(physical(row), PAD, stride=ROWS)
        values = jnp.concatenate([nat[g, at, :] for g in range(GROUPS)], axis=1)
        put_shifts(sh1, 2 + row, activate(values, g1[...].reshape(1, C)))

    own_row(0)
    own_row(1)
    pl.semaphore_wait(barrier, 2 + len(along_z) + len(along_x) + len(along_y))
    to_near = pltpu.make_async_remote_copy(
        src_ref=sh1.at[2, pl.ds(2 + 2 * edge, 2)], dst_ref=near, send_sem=halo_send.at[0], recv_sem=halo_recv.at[0],
        device_id={"span": pos, "tile": partner}, device_id_type=MESH,
    )
    to_near.start()
    for other in along_x:
        pl.semaphore_signal(lines_sem, inc=1, device_id={"span": other, "tile": tile}, device_id_type=MESH)
    own_row(2)
    own_row(3)
    to_far = pltpu.make_async_remote_copy(
        src_ref=sh1.at[2, pl.ds(4, 2)], dst_ref=far, send_sem=halo_send.at[1], recv_sem=halo_recv.at[1],
        device_id={"span": pos, "tile": opposite}, device_id_type=MESH,
    )

    @pl.when(edge == 0)
    def _():
        to_far.start()

    inputs[2].wait()
    inputs[3].wait()
    table = slotv[...]
    lane = lax.broadcasted_iota(jnp.int32, (FRAMES, SPAN), 1)
    column = jnp.sum(jnp.where(lane == pos, table, 0), axis=1, keepdims=True)
    target = jnp.where(column >= 0, column // WSLOT, -1)
    wide_lane = lax.broadcasted_iota(jnp.int32, (FRAMES, 128), 1)
    frame = lax.broadcasted_iota(jnp.int32, (FRAMES, 128), 0)
    pick = jnp.max(jnp.where(target == wide_lane, frame, 0), axis=0, keepdims=True)
    pickv[...] = jnp.broadcast_to(pick, (8, 128))
    wanted = pos * WSLOT + lax.broadcasted_iota(jnp.int32, (WSLOT, SPAN), 0)
    clip = lax.broadcasted_iota(jnp.int32, (WSLOT, SPAN), 1)
    found = jnp.zeros((WSLOT, SPAN), jnp.int32)
    for f in range(FRAMES):
        found = jnp.where(table[f : f + 1, :] == wanted, clip, found)
    srcv[...] = jnp.broadcast_to(jnp.max(found, axis=1, keepdims=True), (WSLOT, 128))
    to_smem = [
        pltpu.make_async_copy(pickv, picks, smem_sem.at[0]),
        pltpu.make_async_copy(srcv, srcs, smem_sem.at[1]),
    ]
    for copy in to_smem:
        copy.start()

    def hidden_row(row, start):
        values = activate(total[start * PAD : (start + 1) * PAD, :].astype(BF16).astype(F32), g2[...].reshape(1, C))
        if row == 0:
            values = jnp.where(edge == 1, 0.0, values)
        put_shifts(sh2, row, values)

    def prepare(half):
        for i in range(2):
            row = physical(2 * half + i)
            for g in range(GROUPS):
                mix[g, pl.ds(lax.rem(row, 2), PAD, stride=2), :] = (
                    nat[g, pl.ds(row, PAD, stride=ROWS), :]
                    + total[i * PAD : (i + 1) * PAD, g * LANES : (g + 1) * LANES]
                )
        for f in range(FRAMES):
            block[half, f] = jnp.concatenate([mix[g, 2 * f : 2 * f + 2, :] for g in range(GROUPS)], axis=1).astype(BF16)
        arrive[half][pos] = block[half, picks[0, pos]]

    def post(half):
        for dy, dx, dz in ORDER:
            dest = shifted_by(dy, dx, dz)
            send[half, dest] = block[half, picks[0, dest]]
            pltpu.make_async_remote_copy(
                src_ref=send.at[half, dest], dst_ref=arrive[half].at[pos],
                send_sem=send_sem.at[half], recv_sem=recv_sem.at[half],
                device_id={"span": dest, "tile": tile}, device_id_type=MESH,
            ).start()

    for copy in weights[TAPS:]:
        copy.start()
    for copy in ahead:
        copy.wait()
    product(sh1, taps((2,), 0), 4, v1, total, 0)
    product(sh1, taps((0,), 4), 2, v1, total, 4)
    for copy in after:
        copy.wait()
    pl.semaphore_wait(lines_sem, len(along_x))
    for other in along_y:
        pl.semaphore_signal(planes_sem, inc=1, device_id={"span": other, "tile": tile}, device_id_type=MESH)

    @pl.when(edge == 1)
    def _():
        sh1[:, 0:2] = jnp.zeros((3, 2, PAD, WIDE), BF16)

    @pl.when(edge == 0)
    def _():
        to_near.wait_recv()
        for row in range(2):
            put_shifts(sh1, row, near[row].astype(F32))

    product(sh1, taps((0, 1), 0), 4, v1, total, 0, add=True)
    for row in range(4):
        hidden_row(row, row)
    for copy in weights[TAPS:]:
        copy.wait()
    product(sh2, taps((0, 1, 2), 0), 2, v2, total, 0)
    for copy in to_smem:
        copy.wait()
    prepare(0)
    pl.semaphore_wait(planes_sem, len(along_y))
    post(0)

    @pl.when(edge == 1)
    def _():
        to_near.wait_recv()
        for row in range(2):
            put_shifts(sh1, 6 + row, near[row].astype(F32))

    @pl.when(edge == 0)
    def _():
        to_far.wait_recv()
        for row in range(2):
            put_shifts(sh1, 7 - row, far[row].astype(F32))

    product(sh1, taps((1, 2), 4), 2, v1, total, 4, add=True)
    hidden_row(4, 4)
    hidden_row(5, 5)
    product(sh2, taps((0, 1, 2), 2), 2, v2, total, 0)
    prepare(1)
    post(1)

    to_near.wait_send()

    @pl.when(edge == 0)
    def _():
        to_far.wait_send()

    every = pl.ds(0, SPAN - 1)
    for half in range(2):
        pltpu.make_async_copy(send.at[half, every], send.at[half, every], send_sem.at[half]).wait()
        pltpu.make_async_copy(arrive[half].at[every], arrive[half].at[every], recv_sem.at[half]).wait()
        for part in range(2):

            @pl.when(flip == (half + part) % 2)
            def _(half=half, part=part):
                for j in range(WSLOT):
                    out[j, 2 * part : 2 * part + 2] = arrive[half][srcs[j, 0]]


def local(features, clip_lengths, slot_table, gain_one, weight_one, gain_two, weight_two):
    del clip_lengths
    hbm = pl.BlockSpec(memory_space=pltpu.HBM)
    operands = [
        features.reshape(FRAMES, ROWS, WIDE),
        slot_table.T,
        gain_one,
        weight_one.reshape(TAPS, 3 * C, C),
        gain_two,
        weight_two.reshape(TAPS, 3 * C, C),
    ]
    operands = [pltpu.with_memory_space_constraint(x, pltpu.HBM) for x in operands]
    return pl.pallas_call(
        kernel,
        out_shape=pltpu.VMEM((WSLOT, ROWS, WIDE), BF16),
        in_specs=[hbm] * 6,
        out_specs=pl.BlockSpec(memory_space=pltpu.VMEM),
        scratch_shapes=[
            pltpu.VMEM((FRAMES, ROWS, WIDE), BF16),
            pltpu.VMEM((FRAMES, SPAN), jnp.int32),
            pltpu.VMEM((C,), F32),
            pltpu.VMEM((C,), F32),
            pltpu.VMEM((GROUPS, ROWS * PAD, LANES), F32),
            pltpu.VMEM((GROUPS, 2 * PAD, LANES), F32),
            pltpu.VMEM((3, 8, PAD, WIDE), BF16),
            pltpu.VMEM((3, 6, PAD, WIDE), BF16),
            pltpu.VMEM((2, PAD, WIDE), BF16),
            pltpu.VMEM((2, PAD, WIDE), BF16),
            pltpu.VMEM((6 * PAD, WIDE), F32),
            pltpu.VMEM((TAPS, 3 * C, C), BF16),
            pltpu.VMEM((TAPS, 3 * C, C), BF16),
            pltpu.VMEM((2, FRAMES, 2, WIDE), BF16),
            pltpu.VMEM((2, SPAN, 2, WIDE), BF16),
            pltpu.VMEM((SPAN, 2, WIDE), BF16),
            pltpu.VMEM((SPAN, 2, WIDE), BF16),
            pltpu.VMEM((8, 128), jnp.int32),
            pltpu.VMEM((WSLOT, 128), jnp.int32),
            pltpu.SMEM((8, 128), jnp.int32),
            pltpu.SMEM((WSLOT, 128), jnp.int32),
            pltpu.SemaphoreType.DMA((4,)),
            pltpu.SemaphoreType.DMA((2, TAPS)),
            pltpu.SemaphoreType.DMA((2,)),
            pltpu.SemaphoreType.DMA((2,)),
            pltpu.SemaphoreType.DMA((2,)),
            pltpu.SemaphoreType.DMA((2,)),
            pltpu.SemaphoreType.DMA((2,)),
            pltpu.SemaphoreType.REGULAR,
            pltpu.SemaphoreType.REGULAR,
        ],
        compiler_params=pltpu.CompilerParams(
            collective_id=0, has_side_effects=True, vmem_limit_bytes=48 * 1024 * 1024
        ),
    )(*operands)


def solution(mesh):
    return jax.shard_map(
        local,
        mesh=mesh,
        in_specs=(P("span", None, "tile", None), P(), P(), P(), P(), P(), P()),
        out_specs=P("span", "tile", None),
        check_vma=False,
    )
```

```python
import functools

import jax
import jax.numpy as jnp
from jax import lax
from jax.experimental import pallas as pl
from jax.experimental.pallas import tpu as pltpu
from jax.sharding import PartitionSpec as P

MESH = pl.DeviceIdType.MESH
FRAMES = 41
PAD = 48
ROWS = 4
C = 384
WIDE = 2 * C
WSLOT = 32
SPAN = 64
TILES = 4
TAPS = 9
ACROSS = 4
DEPTH = 8
XY = ((1, 2), (0, 2), (1, 1), (1, 3), (0, 1), (0, 3), (1, 0), (0, 0))
ORDER = [(dy, dx, dz) for dy, dx in XY for dz in (4, 3, 5, 2, 6, 1, 7)] + [(dy, dx, 0) for dy, dx in XY[:-1]]
LANES = 128
GROUPS = WIDE // LANES
F32 = jnp.float32
BF16 = jnp.bfloat16


def activate(values, gain):
    def half(x):
        u = x * lax.rsqrt(jnp.mean(x * x, axis=-1, keepdims=True) + 1e-06) * gain
        half_u = 0.5 * u
        return half_u + half_u * jnp.tanh(half_u)

    return jnp.concatenate([half(values[:, :C]), half(values[:, C:])], axis=1)


def put_shifts(shifted, row, values):
    frame = lax.broadcasted_iota(jnp.int32, values.shape, 0)
    shifted[2, row] = values.astype(BF16)
    shifted[1, row] = jnp.where(frame >= 1, pltpu.roll(values, 1, 0), 0.0).astype(BF16)
    shifted[0, row] = jnp.where(frame >= 2, pltpu.roll(values, 2, 0), 0.0).astype(BF16)


def product(shifted, pieces, rows, weight, total, start, add=False):
    size = rows * PAD
    lhs = jnp.concatenate(
        [shifted[a, first : first + rows].reshape(size, WIDE) for a, b, first in pieces], axis=1
    )
    for block in range(3):
        rhs = []
        for a, b, _ in pieces:
            tap = a * 3 + b
            if block == 0:
                rhs.append(weight[tap, C:, 0:256])
            elif block == 1:
                rhs.append(jnp.concatenate([weight[tap, C:, 256:], weight[tap, : 2 * C, :128]], axis=1))
            else:
                rhs.append(weight[tap, : 2 * C, 128:])
        result = jnp.dot(lhs, jnp.concatenate(rhs, axis=0), preferred_element_type=F32)
        at = (slice(start * PAD, start * PAD + size), slice(block * 256, (block + 1) * 256))
        total[at] = total[at] + result if add else result


def taps(row_taps, first):
    return [(a, b, first + b) for a in range(3) for b in row_taps]


def kernel(
    feat, slots, gain_one, w_one, gain_two, w_two, out,
    raw, slotv, g1, g2, nat, mix, sh1, sh2, near, far, total, v1, v2, block, send, arrive_one, arrive_two, pickv, srcv, picks, srcs,
    in_sem, w_sem, smem_sem, halo_send, halo_recv, send_sem, recv_sem, lines_sem, planes_sem,
):
    pos = lax.axis_index("span")
    tile = lax.axis_index("tile")
    flip = tile // 2
    arrive = (arrive_one, arrive_two)
    edge = jnp.where((tile == 0) | (tile == TILES - 1), 1, 0)
    partner = tile + 1 - 2 * lax.rem(tile, 2)
    opposite = TILES - 1 - tile

    def physical(row):
        return row + flip * (ROWS - 1 - 2 * row)

    inputs = [
        pltpu.make_async_copy(feat, raw, in_sem.at[0]),
        pltpu.make_async_copy(gain_one, g1, in_sem.at[1]),
        pltpu.make_async_copy(slots, slotv, in_sem.at[2]),
        pltpu.make_async_copy(gain_two, g2, in_sem.at[3]),
    ]
    weights = []
    for which, (src, dst) in enumerate(((w_one, v1), (w_two, v2))):
        for a in range(3):
            for b in range(3):
                tap = a * 3 + b + flip * (2 - 2 * b)
                weights.append(pltpu.make_async_copy(src.at[tap], dst.at[a * 3 + b], w_sem.at[which, a * 3 + b]))
    for copy in inputs[:2]:
        copy.start()

    z, x, y = lax.rem(pos, DEPTH), lax.rem(pos // DEPTH, ACROSS), pos // (DEPTH * ACROSS)

    def shifted_by(dy, dx, dz):
        return (lax.rem(y + dy, 2) * ACROSS + lax.rem(x + dx, ACROSS)) * DEPTH + lax.rem(z + dz, DEPTH)

    barrier = pltpu.get_barrier_semaphore()
    along_z = [shifted_by(0, 0, k) for k in range(1, DEPTH)]
    along_x = [shifted_by(0, k, 0) for k in range(1, ACROSS)]
    along_y = [shifted_by(1, 0, 0)]
    for other in (partner, opposite):
        pl.semaphore_signal(barrier, inc=1, device_id={"span": pos, "tile": other}, device_id_type=MESH)
    for other in along_z + along_x + along_y:
        pl.semaphore_signal(barrier, inc=1, device_id={"span": other, "tile": tile}, device_id_type=MESH)
    ahead, after = weights[2:TAPS:3] + weights[0:TAPS:3], weights[1:TAPS:3]
    for copy in ahead + after + inputs[2:]:
        copy.start()

    inputs[0].wait()
    inputs[1].wait()
    for f in range(FRAMES):
        values = raw[f].astype(F32)
        for g in range(GROUPS):
            nat[g, ROWS * f : ROWS * (f + 1), :] = values[:, g * LANES : (g + 1) * LANES]
    nat[:, ROWS * FRAMES : ROWS * PAD, :] = jnp.zeros((GROUPS, ROWS * (PAD - FRAMES), LANES), F32)

    def own_row(step):
        row = lax.rem(step + 2 * edge, ROWS)
        at = pl.ds(physical(row), PAD, stride=ROWS)
        values = jnp.concatenate([nat[g, at, :] for g in range(GROUPS)], axis=1)
        put_shifts(sh1, 2 + row, activate(values, g1[...].reshape(1, C)))

    own_row(0)
    own_row(1)
    pl.semaphore_wait(barrier, 2 + len(along_z) + len(along_x) + len(along_y))
    to_near = pltpu.make_async_remote_copy(
        src_ref=sh1.at[2, pl.ds(2 + 2 * edge, 2)], dst_ref=near, send_sem=halo_send.at[0], recv_sem=halo_recv.at[0],
        device_id={"span": pos, "tile": partner}, device_id_type=MESH,
    )
    to_near.start()
    for other in along_x:
        pl.semaphore_signal(lines_sem, inc=1, device_id={"span": other, "tile": tile}, device_id_type=MESH)
    own_row(2)
    own_row(3)
    to_far = pltpu.make_async_remote_copy(
        src_ref=sh1.at[2, pl.ds(4, 2)], dst_ref=far, send_sem=halo_send.at[1], recv_sem=halo_recv.at[1],
        device_id={"span": pos, "tile": opposite}, device_id_type=MESH,
    )

    @pl.when(edge == 0)
    def _():
        to_far.start()


    def hidden_row(row, start):
        values = activate(total[start * PAD : (start + 1) * PAD, :].astype(BF16).astype(F32), g2[...].reshape(1, C))
        if row == 0:
            values = jnp.where(edge == 1, 0.0, values)
        put_shifts(sh2, row, values)

    def prepare(half):
        for i in range(2):
            row = physical(2 * half + i)
            for g in range(GROUPS):
                mix[g, pl.ds(lax.rem(row, 2), PAD, stride=2), :] = (
                    nat[g, pl.ds(row, PAD, stride=ROWS), :]
                    + total[i * PAD : (i + 1) * PAD, g * LANES : (g + 1) * LANES]
                )
        for f in range(FRAMES):
            block[half, f] = jnp.concatenate([mix[g, 2 * f : 2 * f + 2, :] for g in range(GROUPS)], axis=1).astype(BF16)
        arrive[half][pos] = block[half, picks[0, pos]]

    def post(half):
        for dy, dx, dz in ORDER:
            dest = shifted_by(dy, dx, dz)
            send[half, dest] = block[half, picks[0, dest]]
            pltpu.make_async_remote_copy(
                src_ref=send.at[half, dest], dst_ref=arrive[half].at[pos],
                send_sem=send_sem.at[half], recv_sem=recv_sem.at[half],
                device_id={"span": dest, "tile": tile}, device_id_type=MESH,
            ).start()

    for copy in weights[TAPS:]:
        copy.start()
    for copy in inputs[2:] + ahead:
        copy.wait()
    table = slotv[...]
    lane = lax.broadcasted_iota(jnp.int32, (FRAMES, SPAN), 1)
    column = jnp.sum(jnp.where(lane == pos, table, 0), axis=1, keepdims=True)
    target = jnp.where(column >= 0, column // WSLOT, -1)
    wide_lane = lax.broadcasted_iota(jnp.int32, (FRAMES, 128), 1)
    frame = lax.broadcasted_iota(jnp.int32, (FRAMES, 128), 0)
    pick = jnp.max(jnp.where(target == wide_lane, frame, 0), axis=0, keepdims=True)
    pickv[...] = jnp.broadcast_to(pick, (8, 128))
    wanted = pos * WSLOT + lax.broadcasted_iota(jnp.int32, (WSLOT, SPAN), 0)
    clip = lax.broadcasted_iota(jnp.int32, (WSLOT, SPAN), 1)
    found = jnp.zeros((WSLOT, SPAN), jnp.int32)
    for f in range(FRAMES):
        found = jnp.where(table[f : f + 1, :] == wanted, clip, found)
    srcv[...] = jnp.broadcast_to(jnp.max(found, axis=1, keepdims=True), (WSLOT, 128))
    product(sh1, taps((2,), 0), 4, v1, total, 0)
    product(sh1, taps((0,), 4), 2, v1, total, 4)
    to_smem = [
        pltpu.make_async_copy(pickv, picks, smem_sem.at[0]),
        pltpu.make_async_copy(srcv, srcs, smem_sem.at[1]),
    ]
    for copy in to_smem:
        copy.start()
    for copy in after:
        copy.wait()
    pl.semaphore_wait(lines_sem, len(along_x))
    for other in along_y:
        pl.semaphore_signal(planes_sem, inc=1, device_id={"span": other, "tile": tile}, device_id_type=MESH)

    @pl.when(edge == 1)
    def _():
        sh1[:, 0:2] = jnp.zeros((3, 2, PAD, WIDE), BF16)

    @pl.when(edge == 0)
    def _():
        to_near.wait_recv()
        for row in range(2):
            put_shifts(sh1, row, near[row].astype(F32))

    product(sh1, taps((0, 1), 0), 4, v1, total, 0, add=True)
    for row in range(4):
        hidden_row(row, row)
    for copy in weights[TAPS:]:
        copy.wait()
    product(sh2, taps((0, 1, 2), 0), 2, v2, total, 0)
    for copy in to_smem:
        copy.wait()
    prepare(0)
    pl.semaphore_wait(planes_sem, len(along_y))
    post(0)

    @pl.when(edge == 1)
    def _():
        to_near.wait_recv()
        for row in range(2):
            put_shifts(sh1, 6 + row, near[row].astype(F32))

    @pl.when(edge == 0)
    def _():
        to_far.wait_recv()
        for row in range(2):
            put_shifts(sh1, 7 - row, far[row].astype(F32))

    product(sh1, taps((1, 2), 4), 2, v1, total, 4, add=True)
    hidden_row(4, 4)
    hidden_row(5, 5)
    product(sh2, taps((0, 1, 2), 2), 2, v2, total, 0)
    prepare(1)
    post(1)

    to_near.wait_send()

    @pl.when(edge == 0)
    def _():
        to_far.wait_send()

    every = pl.ds(0, SPAN - 1)
    for half in range(2):
        pltpu.make_async_copy(send.at[half, every], send.at[half, every], send_sem.at[half]).wait()
        pltpu.make_async_copy(arrive[half].at[every], arrive[half].at[every], recv_sem.at[half]).wait()
        for part in range(2):

            @pl.when(flip == (half + part) % 2)
            def _(half=half, part=part):
                for j in range(WSLOT):
                    out[j, 2 * part : 2 * part + 2] = arrive[half][srcs[j, 0]]


def local(features, clip_lengths, slot_table, gain_one, weight_one, gain_two, weight_two):
    del clip_lengths
    hbm = pl.BlockSpec(memory_space=pltpu.HBM)
    operands = [
        features.reshape(FRAMES, ROWS, WIDE),
        slot_table.T,
        gain_one,
        weight_one.reshape(TAPS, 3 * C, C),
        gain_two,
        weight_two.reshape(TAPS, 3 * C, C),
    ]
    operands = [pltpu.with_memory_space_constraint(x, pltpu.HBM) for x in operands]
    return pl.pallas_call(
        kernel,
        out_shape=pltpu.VMEM((WSLOT, ROWS, WIDE), BF16),
        in_specs=[hbm] * 6,
        out_specs=pl.BlockSpec(memory_space=pltpu.VMEM),
        scratch_shapes=[
            pltpu.VMEM((FRAMES, ROWS, WIDE), BF16),
            pltpu.VMEM((FRAMES, SPAN), jnp.int32),
            pltpu.VMEM((C,), F32),
            pltpu.VMEM((C,), F32),
            pltpu.VMEM((GROUPS, ROWS * PAD + 8, LANES), F32),
            pltpu.VMEM((GROUPS, 2 * PAD + 8, LANES), F32),
            pltpu.VMEM((3, 8, PAD, WIDE), BF16),
            pltpu.VMEM((3, 6, PAD, WIDE), BF16),
            pltpu.VMEM((2, PAD, WIDE), BF16),
            pltpu.VMEM((2, PAD, WIDE), BF16),
            pltpu.VMEM((6 * PAD, WIDE), F32),
            pltpu.VMEM((TAPS, 3 * C, C), BF16),
            pltpu.VMEM((TAPS, 3 * C, C), BF16),
            pltpu.VMEM((2, FRAMES, 2, WIDE), BF16),
            pltpu.VMEM((2, SPAN, 2, WIDE), BF16),
            pltpu.VMEM((SPAN, 2, WIDE), BF16),
            pltpu.VMEM((SPAN, 2, WIDE), BF16),
            pltpu.VMEM((8, 128), jnp.int32),
            pltpu.VMEM((WSLOT, 128), jnp.int32),
            pltpu.SMEM((8, 128), jnp.int32),
            pltpu.SMEM((WSLOT, 128), jnp.int32),
            pltpu.SemaphoreType.DMA((4,)),
            pltpu.SemaphoreType.DMA((2, TAPS)),
            pltpu.SemaphoreType.DMA((2,)),
            pltpu.SemaphoreType.DMA((2,)),
            pltpu.SemaphoreType.DMA((2,)),
            pltpu.SemaphoreType.DMA((2,)),
            pltpu.SemaphoreType.DMA((2,)),
            pltpu.SemaphoreType.REGULAR,
            pltpu.SemaphoreType.REGULAR,
        ],
        compiler_params=pltpu.CompilerParams(
            collective_id=0, has_side_effects=True, vmem_limit_bytes=48 * 1024 * 1024
        ),
    )(*operands)


def solution(mesh):
    return jax.shard_map(
        local,
        mesh=mesh,
        in_specs=(P("span", None, "tile", None), P(), P(), P(), P(), P(), P()),
        out_specs=P("span", "tile", None),
        check_vma=False,
    )
```
